32 devices in a mesh: row: 4 (over y, x), col: 8 (over z, core).
Axes of the slice: x: 2, y: 2, z: 4, core: 2. Of those that a mesh axis runs over, the one named last changes fastest.
Arguments:
- intensity: int32 [128, 2048], P('row', 'col'), may hold values from 0 to 255
- agreement: int32 [4, 128, 2048], P(None, 'row', 'col'), may hold values from 0 to 8
- basis_block: float32 [128, 128, 2048], P(None, 'row', 'col'), may hold values from -2000 to 2000
Outputs:
- ortho_block: float32 [128, 128, 2048], P(None, 'row', 'col')
- upper_factor: float32 [128, 128], replicated
The draws below stay inside these ranges and needn't reach their ends.
All inputs are finite; a program needn't handle non-finite values.
Results may differ from the reference program's by a relative error of at most 0.00014.
Values sent between devices are 32-bit elements; how exact they have to be, the bound alone decides.
A program may use at most 64 MiB of HBM per device.

```python
import math
import jax
import jax.numpy as jnp
from jax import lax

K = 128
NR = 128
NC = 2048


def draw_basis_block(key, part):
    first, second, third = jax.random.split(key, 3)
    vector_scale = jnp.exp(jax.random.uniform(second, (K, 1, 1), jnp.float32, 0.0, math.log(10.0)))
    pixel_scale = jnp.exp(jax.random.uniform(third, (1, NR, NC), jnp.float32, 0.0, math.log(10.0)))
    row_pos = jnp.arange(NR, dtype=jnp.float32)[:, None] / NR
    col_pos = jnp.arange(NC, dtype=jnp.float32)[None, :] / NC
    trend = jnp.exp(0.5 * math.log(3.0) * (row_pos + col_pos))[None]
    base = jnp.clip(jax.random.normal(first, (K, NR, NC), jnp.float32), -6.0, 6.0)
    return (base * vector_scale * pixel_scale * trend).astype(jnp.float32)


def plant(values, rng, least, top_value):
    place = [jax.random.randint(jax.random.fold_in(rng, axis), (), 0, length) for axis, length in enumerate(values.shape)]
    main_axis = values.shape.index(max(values.shape))
    beside = place[:main_axis] + [(place[main_axis] + 1) % values.shape[main_axis]] + place[main_axis + 1:]
    return values.at[tuple(place)].set(least).at[tuple(beside)].set(top_value)


def setup_inputs(seed: int = 0) -> dict:
    seeds = jax.random.split(jax.random.key(seed), 4)
    return {
        "intensity": plant(jax.random.randint(seeds[0], (NR, NC), 0, 256), jax.random.fold_in(seeds[0], 1), 0, 255).astype(jnp.int32),
        "agreement": plant(jax.random.randint(seeds[1], (4, NR, NC), 0, 9), jax.random.fold_in(seeds[1], 1), 0, 8).astype(jnp.int32),
        "basis_block": draw_basis_block(jax.random.fold_in(seeds[3], 71), 0),
    }


INV_SIGMA = 1.0 / 40.0
NEIGHBOURS = ((0, 1, 0, 1, 1.0 / 9.0), (0, -1, 0, 0, 1.0 / 9.0), (1, 0, 1, 1, 1.0 / 9.0), (-1, 0, 1, 0, 1.0 / 9.0), (1, 1, 2, 1, 1.0 / 18.0), (-1, -1, 2, 0, 1.0 / 18.0), (1, -1, 3, 1, 1.0 / 18.0), (-1, 1, 3, 0, 1.0 / 18.0))

def shifted(array, step_row, step_col):
    height = array.shape[-2]
    width = array.shape[-1]
    return array[..., 1 + step_row:height - 1 + step_row, 1 + step_col:width - 1 + step_col]

def cropped(array, cycle):
    if cycle == 0:
        return array
    return array[..., cycle:-cycle, cycle:-cycle]

def neighbour_weights(levels, counts, inside):
    center = shifted(levels, 0, 0)
    center_in = shifted(inside, 0, 0)
    result = []
    for step_row, step_col, channel, at_center, factor in NEIGHBOURS:
        other = shifted(levels, step_row, step_col)
        if at_center == 1:
            source = shifted(counts[channel], 0, 0)
        else:
            source = shifted(counts[channel], step_row, step_col)
        gap = (center - other) * INV_SIGMA
        result.append((1.0 + source) * factor * jnp.exp(-gap * gap) * center_in * shifted(inside, step_row, step_col))
    return result

def degree_scales(weights):
    degree = weights[0]
    for weight in weights[1:]:
        degree = degree + weight
    return lax.rsqrt(1.0 + degree)

def apply_once(values_in, weights, scales):
    lifted = values_in * scales
    summed = None
    for weight, entry in zip(weights, NEIGHBOURS):
        term = weight * shifted(lifted, entry[0], entry[1])
        summed = term if summed is None else summed + term
    return shifted(values_in, 0, 0) - shifted(scales, 0, 0) * summed

def reference(intensity, agreement, basis_block):
    levels = jnp.pad(intensity.astype(jnp.float32), 3)
    counts = jnp.pad(agreement.astype(jnp.float32), ((0, 0), (3, 3), (3, 3)))
    inside = jnp.pad(jnp.ones((NR, NC), jnp.float32), 3)
    weights = neighbour_weights(levels, counts, inside)
    scales = degree_scales(weights)
    inner_weights = [cropped(weight, 2) for weight in weights]
    inner_scales = cropped(scales, 1)

    def apply_group(group):
        padded = jnp.pad(group, ((0, 0), (1, 1), (1, 1)))
        first = apply_once(padded, inner_weights, inner_scales)
        padded = jnp.pad(first, ((0, 0), (1, 1), (1, 1)))
        return apply_once(padded, inner_weights, inner_scales)
    groups = basis_block.reshape(K // 8, 8, NR, NC)
    filtered = lax.map(apply_group, groups).reshape(K, NR * NC)
    gram = jnp.dot(filtered.astype(jnp.float32), filtered.T.astype(jnp.float32), precision=lax.Precision.HIGHEST, preferred_element_type=jnp.float32) / float(NR * NC)
    factor = jnp.linalg.cholesky(gram)
    ortho = jax.scipy.linalg.solve_triangular(factor, filtered, lower=True)
    return (ortho.reshape(K, NR, NC), factor.T)
```

```python
import jax
import jax.numpy as jnp
from jax import lax
from jax.experimental import pallas as pl
from jax.experimental.pallas import tpu as pltpu
from jax.sharding import PartitionSpec as P

INV_SIGMA = 1.0 / 40.0
NEIGHBOURS = (
    (0, 1, 0, 1, 1.0 / 9.0),
    (0, -1, 0, 0, 1.0 / 9.0),
    (1, 0, 1, 1, 1.0 / 9.0),
    (-1, 0, 1, 0, 1.0 / 9.0),
    (1, 1, 2, 1, 1.0 / 18.0),
    (-1, -1, 2, 0, 1.0 / 18.0),
    (1, -1, 3, 1, 1.0 / 18.0),
    (-1, 1, 3, 0, 1.0 / 18.0),
)
PANEL = 16


def padded(cells, sides, width):
    for axis, dim in sides:
        count = lax.axis_size(axis)
        ends = count - 1
        head = lax.slice_in_dim(cells, 0, width, axis=dim)
        tail = lax.slice_in_dim(cells, cells.shape[dim] - width, cells.shape[dim], axis=dim)
        cells = jnp.concatenate(
            [
                lax.ppermute(tail, axis, [(i, (i + 1) % count) for i in range(ends)]),
                cells,
                lax.ppermute(head, axis, [((i + 1) % count, i) for i in range(ends)]),
            ],
            axis=dim,
        )
    return cells


def shifted(array, step_row, step_col):
    height = array.shape[-2]
    width = array.shape[-1]
    return array[..., 1 + step_row : height - 1 + step_row, 1 + step_col : width - 1 + step_col]


def cropped(array, cycle):
    return array[..., cycle:-cycle, cycle:-cycle]


def neighbour_weights(levels, counts, inside):
    center = shifted(levels, 0, 0)
    center_in = shifted(inside, 0, 0)
    result = []
    for step_row, step_col, channel, at_center, factor in NEIGHBOURS:
        other = shifted(levels, step_row, step_col)
        if at_center == 1:
            source = shifted(counts[channel], 0, 0)
        else:
            source = shifted(counts[channel], step_row, step_col)
        gap = (center - other) * INV_SIGMA
        result.append(
            (1.0 + source)
            * factor
            * jnp.exp(-gap * gap)
            * center_in
            * shifted(inside, step_row, step_col)
        )
    return result


def degree_scales(weights):
    degree = weights[0]
    for weight in weights[1:]:
        degree = degree + weight
    return lax.rsqrt(1.0 + degree)


def apply_once(values_in, weights, scales):
    lifted = values_in * scales
    summed = None
    for weight, entry in zip(weights, NEIGHBOURS):
        term = weight * shifted(lifted, entry[0], entry[1])
        summed = term if summed is None else summed + term
    return shifted(values_in, 0, 0) - shifted(scales, 0, 0) * summed


def inner_products(first_mat, second_mat):
    return jnp.dot(
        first_mat, second_mat.T, precision=lax.Precision.HIGHEST, preferred_element_type=jnp.float32
    )


def factor_panels(work):
    size, width = work.shape
    for base in range(0, size, PANEL):
        block = work[pl.ds(base, PANEL), :]
        rows = [block[i : i + 1, :] for i in range(PANEL)]
        pivots = [
            [
                None
                if k < i
                else jnp.broadcast_to(rows[i][:, base + k : base + k + 1], (1, width))
                for k in range(PANEL)
            ]
            for i in range(PANEL)
        ]
        for i in range(PANEL):
            inverse = lax.rsqrt(pivots[i][i])
            rows[i] = rows[i] * inverse
            lead = [None if k <= i else pivots[i][k] * inverse for k in range(PANEL)]
            for k in range(i + 1, PANEL):
                for m in range(k, PANEL):
                    pivots[k][m] = pivots[k][m] - lead[k] * lead[m]
            for k in range(i + 1, PANEL):
                rows[k] = rows[k] - lead[k] * rows[i]
        done = jnp.concatenate(rows, axis=0)
        work[pl.ds(base, PANEL), :] = done
        rest = size - base - PANEL
        if rest > 0:
            change = lax.dot_general(
                done[:, :size].T,
                done,
                (((1,), (0,)), ((), ())),
                precision=lax.Precision.HIGHEST,
                preferred_element_type=jnp.float32,
            )
            work[pl.ds(base + PANEL, rest), :] = (
                work[pl.ds(base + PANEL, rest), :] - change[base + PANEL :, :]
            )


def split_two(values):
    high = values.astype(jnp.bfloat16)
    low = (values - high.astype(jnp.float32)).astype(jnp.bfloat16)
    return high, low


def ortho_kernel(scale, gram_ref, filt_ref, ortho_ref, upper_ref, work, filt, out, in_sem, out_sem):
    size = gram_ref.shape[0]
    rows = filt.shape[0]
    fetch = pltpu.make_async_copy(filt_ref, filt, in_sem)
    fetch.start()
    row_id = lax.broadcasted_iota(jnp.int32, (size, size), 0)
    col_id = lax.broadcasted_iota(jnp.int32, (size, size), 1)
    work[:, :size] = gram_ref[...] * scale
    work[:, size:] = jnp.where(row_id == col_id, 1.0, 0.0).astype(jnp.float32)
    factor_panels(work)
    upper_ref[...] = jnp.where(row_id <= col_id, work[:, :size], 0.0)
    high, low = split_two(work[:, size:])
    left = jnp.concatenate(
        [jnp.concatenate([high, high], axis=1), jnp.concatenate([low, low], axis=1)], axis=0
    )
    fetch.wait()
    sends = []
    for group in range(rows // 8):
        parts = []
        for r in range(8):
            pair = jnp.concatenate(split_two(filt[group * 8 + r]), axis=0)
            both = jnp.dot(left, pair, preferred_element_type=jnp.float32)
            parts.append(both[:size] + both[size:])
        out[:, pl.ds(group * 8, 8), :] = jnp.swapaxes(jnp.stack(parts, axis=0), 0, 1)
        send = pltpu.make_async_copy(
            out.at[:, pl.ds(group * 8, 8), :],
            ortho_ref.at[:, pl.ds(group * 8, 8), :],
            out_sem.at[group],
        )
        send.start()
        sends.append(send)
    for send in sends:
        send.wait()


def ortho_call(gram, filt, pixels):
    rows, vectors, cols = filt.shape

    def body(*refs):
        ortho_kernel(1.0 / pixels, *refs)

    return pl.pallas_call(
        body,
        out_shape=(
            jax.ShapeDtypeStruct((vectors, rows, cols), jnp.float32),
            jax.ShapeDtypeStruct((vectors, vectors), jnp.float32),
        ),
        in_specs=[
            pl.BlockSpec(memory_space=pltpu.VMEM),
            pl.BlockSpec(memory_space=pl.ANY),
        ],
        out_specs=(
            pl.BlockSpec(memory_space=pl.ANY),
            pl.BlockSpec(memory_space=pltpu.VMEM),
        ),
        scratch_shapes=[
            pltpu.VMEM((vectors, 2 * vectors), jnp.float32),
            pltpu.VMEM((rows, vectors, cols), filt.dtype),
            pltpu.VMEM((vectors, rows, cols), jnp.float32),
            pltpu.SemaphoreType.DMA,
            pltpu.SemaphoreType.DMA((rows // 8,)),
        ],
        compiler_params=pltpu.CompilerParams(vmem_limit_bytes=40 * 1024 * 1024),
        name="ortho",
    )(gram, filt)


def per_device(intensity, agreement, basis_block):
    vectors, tile_rows, tile_cols = basis_block.shape
    row_count = lax.axis_size("row")
    col_count = lax.axis_size("col")
    total_rows = tile_rows * row_count
    total_cols = tile_cols * col_count
    labels = jnp.concatenate((intensity[None], agreement), axis=0)
    labels_wide = padded(labels, (("row", 1), ("col", 2)), 3)
    row_ids = lax.axis_index("row") * tile_rows + jnp.arange(-3, tile_rows + 3, dtype=jnp.int32)
    col_ids = lax.axis_index("col") * tile_cols + jnp.arange(-3, tile_cols + 3, dtype=jnp.int32)
    row_in = ((row_ids >= 0) & (row_ids < total_rows)).astype(jnp.float32)
    col_in = ((col_ids >= 0) & (col_ids < total_cols)).astype(jnp.float32)
    inside = row_in[:, None] * col_in[None, :]
    levels = labels_wide[0].astype(jnp.float32)
    counts = labels_wide[1:].astype(jnp.float32)
    weights = neighbour_weights(levels, counts, inside)
    scales = degree_scales(weights)
    cycle_zero = [cropped(weight, 2) for weight in weights]
    filtered = basis_block
    for repeat in range(2):
        extended = padded(filtered, (("row", 1), ("col", 2)), 1)
        filtered = apply_once(extended, cycle_zero, cropped(scales, 1))
    flat = filtered.reshape(vectors, tile_rows * tile_cols)
    gram = lax.psum(inner_products(flat, flat), ("row", "col"))
    return ortho_call(gram, filtered.swapaxes(0, 1), float(total_rows * total_cols))


def solution(mesh):
    return jax.shard_map(
        per_device,
        mesh=mesh,
        in_specs=(P("row", "col"), P(None, "row", "col"), P(None, "row", "col")),
        out_specs=(P(None, "row", "col"), P()),
        check_vma=False,
    )
```

```python
import jax
import jax.numpy as jnp
from jax import lax
from jax.experimental import pallas as pl
from jax.experimental.pallas import tpu as pltpu
from jax.sharding import PartitionSpec as P

INV_SIGMA = 1.0 / 40.0
NEIGHBOURS = (
    (0, 1, 0, 1, 1.0 / 9.0),
    (0, -1, 0, 0, 1.0 / 9.0),
    (1, 0, 1, 1, 1.0 / 9.0),
    (-1, 0, 1, 0, 1.0 / 9.0),
    (1, 1, 2, 1, 1.0 / 18.0),
    (-1, -1, 2, 0, 1.0 / 18.0),
    (1, -1, 3, 1, 1.0 / 18.0),
    (-1, 1, 3, 0, 1.0 / 18.0),
)
PANEL = 16


DIRECTIONS = ((-1, 0), (1, 0), (0, -1), (0, 1), (-1, -1), (-1, 1), (1, -1), (1, 1))
STEPS = ((-1, -1), (0, -1), (1, -1), (-1, 1), (0, 1), (1, 1), (-1, 0), (1, 0))
CHUNK = 16
LANES = 128
EDGE = 8


def moved(array, step_row, step_col):
    height, width = array.shape
    if step_row:
        array = pltpu.roll(array, (-step_row) % height, 0)
    if step_col:
        array = pltpu.roll(array, (-step_col) % width, 1)
    return array


def stencil_weights(levels_ref, counts_ref, weights, row, col, row_count, col_count):
    height, width = levels_ref.shape
    rows, cols = height - 2 * EDGE, width - 2 * LANES
    row_id = lax.broadcasted_iota(jnp.int32, (height, width), 0) - EDGE + row * rows
    col_id = lax.broadcasted_iota(jnp.int32, (height, width), 1) - LANES + col * cols
    total_rows, total_cols = rows * row_count, cols * col_count

    def is_inside(step_row, step_col):
        r, c = row_id + step_row, col_id + step_col
        return (r >= 0) & (r < total_rows) & (c >= 0) & (c < total_cols)

    center_in = is_inside(0, 0)
    levels = levels_ref[...].astype(jnp.float32)
    edges = {}
    for step_row, step_col, channel, at_center, factor in NEIGHBOURS:
        if at_center == 1:
            gap = (levels - moved(levels, step_row, step_col)) * INV_SIGMA
            count = counts_ref[channel].astype(jnp.float32)
            weight = (1.0 + count) * factor * jnp.exp(-gap * gap)
            edges[channel] = (
                jnp.where(center_in & is_inside(step_row, step_col), weight, 0.0),
                (step_row, step_col),
            )
    degree = None
    for step_row, step_col, channel, at_center, factor in NEIGHBOURS:
        weight = edges[channel][0]
        if at_center == 0:
            weight = moved(weight, step_row, step_col)
        degree = weight if degree is None else degree + weight
    scales = lax.rsqrt(1.0 + degree)
    table = {}
    for step_row, step_col, channel, at_center, factor in NEIGHBOURS:
        if at_center == 1:
            scaled = edges[channel][0] * scales * moved(scales, step_row, step_col)
            table[(step_row, step_col)] = scaled
            table[(-step_row, -step_col)] = moved(scaled, -step_row, -step_col)
    lane = lax.broadcasted_iota(jnp.int32, (height, LANES), 1)
    for n, (step_row, step_col) in enumerate(STEPS):
        weight = moved(table[(step_row, step_col)], 0, -step_col)
        weights[n, :, :cols] = weight[:, LANES : LANES + cols]
        weights[n, :, cols:] = jnp.where(
            lane < LANES // 2, weight[:, LANES + cols :], weight[:, :LANES]
        )


def apply_row(source, at, weights, weight_row, store):
    vectors, width = source.shape[1], source.shape[2]
    parts = [weights[n, pl.ds(weight_row, 1), :] for n in range(len(STEPS))]
    for base in range(0, vectors, CHUNK):
        above = source[at - 1, base : base + CHUNK, :]
        here = source[at, base : base + CHUNK, :]
        below = source[at + 1, base : base + CHUNK, :]
        from_left = parts[0] * above + parts[1] * here + parts[2] * below
        from_right = parts[3] * above + parts[4] * here + parts[5] * below
        upright = parts[6] * above + parts[7] * below
        store(
            base,
            here - (upright + pltpu.roll(from_left, 1, 1) + pltpu.roll(from_right, width - 1, 1)),
        )


def filter_kernel(
    row_count,
    col_count,
    levels_in,
    counts_in,
    basis_in,
    pair_out,
    gram_out,
    levels,
    counts,
    natural,
    wide,
    middle,
    weights,
    packed,
    halo,
    pairs,
    total,
    share,
    landed,
    blocks,
    whole,
    local_sem,
    send_sem,
    recv_sem,
    sum_send,
    sum_recv,
):
    vectors, rows, cols = natural.shape
    width = cols + LANES
    row, col = lax.axis_index("row"), lax.axis_index("col")

    def device(step_row, step_col):
        return {
            "row": jnp.clip(row + step_row, 0, row_count - 1),
            "col": jnp.clip(col + step_col, 0, col_count - 1),
        }

    def exists(step_row, step_col):
        r, c = row + step_row, col + step_col
        return (r >= 0) & (r < row_count) & (c >= 0) & (c < col_count)

    groups = rows // 8
    order = [0, groups - 1] + list(range(1, groups - 1))
    fetches = {}
    for g in order:
        fetches[g] = pltpu.make_async_copy(
            basis_in.at[:, pl.ds(8 * g, 8), :],
            natural.at[:, pl.ds(8 * g, 8), :],
            local_sem.at[g],
        )
        fetches[g].start()
    own = [
        pltpu.make_async_copy(
            levels_in, levels.at[pl.ds(EDGE, rows), pl.ds(LANES, cols)], local_sem.at[groups]
        ),
        pltpu.make_async_copy(
            counts_in, counts.at[:, pl.ds(EDGE, rows), pl.ds(LANES, cols)], local_sem.at[groups + 1]
        ),
    ]
    for copy in own:
        copy.start()
    zeros = jnp.zeros((2, vectors, cols), jnp.float32)
    wide[0:2, :, :cols] = zeros
    wide[rows + 2 : rows + 4, :, :cols] = zeros
    halo[...] = jnp.zeros(halo.shape, jnp.float32)

    barrier = pltpu.get_barrier_semaphore()

    def greet(target):
        pl.semaphore_signal(
            barrier, inc=1, device_id=target, device_id_type=pl.DeviceIdType.MESH
        )

    for off in range(1, col_count):
        greet({"row": row, "col": lax.rem(col + off, col_count)})
    for off in range(1, row_count):
        greet({"row": lax.rem(row + off, row_count), "col": col})
    corners = jnp.int32(0)
    for step in DIRECTIONS[4:]:
        corners = corners + jnp.where(exists(*step), 1, 0)

        @pl.when(exists(*step))
        def _(step=step):
            greet(device(*step))

    pl.semaphore_wait(barrier, col_count + row_count - 2 + corners)

    def span(step, size, edge):
        if step == 0:
            return 0, edge, size
        if step == 1:
            return size - edge, 0, edge
        return 0, edge + size, edge

    def remote(source, target, kind, d):
        return pltpu.make_async_remote_copy(
            src_ref=source,
            dst_ref=target,
            send_sem=send_sem.at[kind, d],
            recv_sem=recv_sem.at[kind, d],
            device_id=device(*DIRECTIONS[d]),
            device_id_type=pl.DeviceIdType.MESH,
        )

    def launch(d, copies):
        @pl.when(exists(*DIRECTIONS[d]))
        def _():
            for copy in copies:
                copy.start()

    def arrive(d, copies):
        @pl.when(exists(-DIRECTIONS[d][0], -DIRECTIONS[d][1]))
        def _():
            for copy in copies:
                copy.wait_recv()

    label_copies = []
    for d, (step_row, step_col) in enumerate(DIRECTIONS):
        r_from, r_to, r_len = span(step_row, rows, EDGE)
        c_from, c_to, c_len = span(step_col, cols, LANES)
        label_copies.append(
            [
                remote(
                    levels_in.at[pl.ds(r_from, r_len), pl.ds(c_from, c_len)],
                    levels.at[pl.ds(r_to, r_len), pl.ds(c_to, c_len)],
                    0,
                    d,
                ),
                remote(
                    counts_in.at[:, pl.ds(r_from, r_len), pl.ds(c_from, c_len)],
                    counts.at[:, pl.ds(r_to, r_len), pl.ds(c_to, c_len)],
                    1,
                    d,
                ),
            ]
        )
        launch(d, label_copies[d])

    def turn(g):
        fetches[g].wait()
        wide[pl.ds(2 + 8 * g, 8), :, pl.ds(0, cols)] = jnp.swapaxes(
            natural[:, pl.ds(8 * g, 8), :], 0, 1
        )

    turn(0)
    value_copies = [None] * 8
    value_copies[0] = [
        remote(wide.at[pl.ds(2, 2), :, pl.ds(0, cols)],
               wide.at[pl.ds(rows + 2, 2), :, pl.ds(0, cols)], 2, 0)
    ]
    launch(0, value_copies[0])
    turn(groups - 1)
    value_copies[1] = [
        remote(wide.at[pl.ds(rows, 2), :, pl.ds(0, cols)],
               wide.at[pl.ds(0, 2), :, pl.ds(0, cols)], 2, 1)
    ]
    launch(1, value_copies[1])
    for g in range(1, groups - 1):
        turn(g)

    lane = lax.broadcasted_iota(jnp.int32, (vectors, LANES), 1)
    used = 2 * rows
    for side, start in ((0, 0), (1, cols - LANES)):
        gathered = jnp.zeros((vectors, LANES), jnp.float32)
        for r in range(rows):
            strip = wide[2 + r, :, start : start + LANES]
            shift = (2 * r + 2 * side) % LANES
            if shift:
                strip = pltpu.roll(strip, shift, 1)
            gathered = jnp.where(lane // 2 == r, strip, gathered)
        packed[side] = gathered.T
    for d, (step_row, step_col) in enumerate(DIRECTIONS):
        if step_col == 0:
            continue
        side = 0 if step_col < 0 else 1
        p_from, p_to, p_len = span(step_row, used, EDGE)
        value_copies[d] = [
            remote(
                packed.at[side, pl.ds(p_from, p_len), :],
                halo.at[1 - side, pl.ds(p_to, p_len), :],
                2,
                d,
            )
        ]
        launch(d, value_copies[d])

    for copy in own:
        copy.wait()
    for d in range(8):
        arrive(d, label_copies[d])
    stencil_weights(levels, counts, weights, row, col, row_count, col_count)

    for d in range(2, 8):
        arrive(d, value_copies[d])
    left, right = halo[0].T, halo[1].T
    for r in range(-2, rows + 2):
        on_right = pltpu.roll(right, (-(EDGE + 2 * r)) % LANES, 1)
        on_left = pltpu.roll(left, (LANES - 2 - EDGE - 2 * r) % LANES, 1)
        wide[2 + r, :, cols:] = jnp.where(lane < LANES // 2, on_right, on_left)

    def first(m):
        def store(base, values):
            middle[m, base : base + CHUNK, :] = values

        apply_row(wide, m + 1, weights, m + EDGE - 1, store)

    def second(r):
        def store(base, values):
            high, low = split_two(values[:, :cols])
            pairs[r, base : base + CHUNK, :] = high
            pairs[r, vectors + base : vectors + base + CHUNK, :] = low

        apply_row(middle, r + 1, weights, r + EDGE, store)

    def product(r):
        pair = pairs[r]
        total[...] += lax.dot_general(
            pair, pair, (((1,), (1,)), ((), ())), preferred_element_type=jnp.float32
        )

    total[...] = jnp.zeros(total.shape, jnp.float32)
    first(2)
    first(3)

    def inner(r, carry):
        first(r + 2)
        second(r)
        return carry

    lax.fori_loop(2, rows - 2, inner, 0)

    def inner_product(r, carry):
        product(r)
        return carry

    lax.fori_loop(2, rows - 2, inner_product, 0)
    for d in range(2):
        arrive(d, value_copies[d])
    for m in (0, 1, rows, rows + 1):
        first(m)
    for r in (0, 1, rows - 2, rows - 1):
        second(r)
    keep = pltpu.make_async_copy(pairs, pair_out, local_sem.at[groups + 2])
    keep.start()
    for r in (0, 1, rows - 2, rows - 1):
        product(r)

    block = vectors // col_count
    share[...] = (total[:vectors, :vectors] + total[vectors:, vectors:]) + (
        total[:vectors, vectors:] + total[vectors:, :vectors]
    )

    def swap(source, target, n, peer):
        copy = pltpu.make_async_remote_copy(
            src_ref=source,
            dst_ref=target,
            send_sem=sum_send.at[n],
            recv_sem=sum_recv.at[n],
            device_id=peer,
            device_id_type=pl.DeviceIdType.MESH,
        )
        copy.start()
        return copy

    def col_peer(off):
        return {"row": row, "col": lax.rem(col + off, col_count)}

    scatter = []
    for off in range(1, col_count):
        place = pl.multiple_of(lax.rem(col + off, col_count) * block, block)
        scatter.append(
            swap(share.at[pl.ds(place, block), :], landed.at[off], off - 1, col_peer(off))
        )
    mine = pl.multiple_of(col * block, block)
    part = share[pl.ds(mine, block), :]
    for off in range(1, col_count):
        scatter[off - 1].wait_recv()
        part = part + landed[off]
    blocks[row] = part
    spread = []
    for off in range(1, row_count):
        spread.append(
            swap(
                blocks.at[row],
                blocks.at[row],
                col_count + off - 1,
                {"row": lax.rem(row + off, row_count), "col": col},
            )
        )
    for copy in spread:
        copy.wait_recv()
    part = blocks[0]
    for n in range(1, row_count):
        part = part + blocks[n]
    whole[pl.ds(mine, block), :] = part
    collect = []
    for off in range(1, col_count):
        collect.append(
            swap(
                whole.at[pl.ds(mine, block), :],
                whole.at[pl.ds(mine, block), :],
                col_count + row_count + off - 1,
                col_peer(off),
            )
        )
    for copy in collect:
        copy.wait_recv()
    gram_out[...] = whole[...]
    for d in range(8):

        @pl.when(exists(*DIRECTIONS[d]))
        def _(d=d):
            for copy in label_copies[d] + value_copies[d]:
                copy.wait_send()

    for copy in scatter + spread + collect:
        copy.wait_send()
    keep.wait()


def filter_call(intensity, agreement, basis_block, row_count, col_count):
    vectors, rows, cols = basis_block.shape
    block = vectors // col_count

    def body(*refs):
        filter_kernel(row_count, col_count, *refs)

    any_spec = pl.BlockSpec(memory_space=pl.ANY)
    f32 = jnp.float32
    swaps = 2 * col_count + row_count
    return pl.pallas_call(
        body,
        out_shape=(
            jax.ShapeDtypeStruct((rows, 2 * vectors, cols), jnp.bfloat16),
            jax.ShapeDtypeStruct((vectors, vectors), f32),
        ),
        in_specs=[any_spec] * 3,
        out_specs=(any_spec, pl.BlockSpec(memory_space=pltpu.VMEM)),
        scratch_shapes=[
            pltpu.VMEM((rows + 2 * EDGE, cols + 2 * LANES), jnp.int32),
            pltpu.VMEM((4, rows + 2 * EDGE, cols + 2 * LANES), jnp.int32),
            pltpu.VMEM((vectors, rows, cols), f32),
            pltpu.VMEM((rows + 4, vectors, cols + LANES), f32),
            pltpu.VMEM((rows + 2, vectors, cols + LANES), f32),
            pltpu.VMEM((len(STEPS), rows + 2 * EDGE, cols + LANES), f32),
            pltpu.VMEM((2, LANES, vectors), f32),
            pltpu.VMEM((2, LANES, vectors), f32),
            pltpu.VMEM((rows, 2 * vectors, cols), jnp.bfloat16),
            pltpu.VMEM((2 * vectors, 2 * vectors), f32),
            pltpu.VMEM((vectors, vectors), f32),
            pltpu.VMEM((col_count, block, vectors), f32),
            pltpu.VMEM((row_count, block, vectors), f32),
            pltpu.VMEM((vectors, vectors), f32),
            pltpu.SemaphoreType.DMA((rows // 8 + 3,)),
            pltpu.SemaphoreType.DMA((3, 8)),
            pltpu.SemaphoreType.DMA((3, 8)),
            pltpu.SemaphoreType.DMA((swaps,)),
            pltpu.SemaphoreType.DMA((swaps,)),
        ],
        compiler_params=pltpu.CompilerParams(
            collective_id=0, has_side_effects=True, vmem_limit_bytes=48 * 1024 * 1024
        ),
        name="filter",
    )(intensity, agreement, basis_block)


def factor_panels(work):
    size, width = work.shape
    for base in range(0, size, PANEL):
        block = work[pl.ds(base, PANEL), :]
        rows = [block[i : i + 1, :] for i in range(PANEL)]
        pivots = [
            [
                None
                if k < i
                else jnp.broadcast_to(rows[i][:, base + k : base + k + 1], (1, width))
                for k in range(PANEL)
            ]
            for i in range(PANEL)
        ]
        for i in range(PANEL):
            inverse = lax.rsqrt(pivots[i][i])
            rows[i] = rows[i] * inverse
            lead = [None if k <= i else pivots[i][k] * inverse for k in range(PANEL)]
            for k in range(i + 1, PANEL):
                for m in range(k, PANEL):
                    pivots[k][m] = pivots[k][m] - lead[k] * lead[m]
            for k in range(i + 1, PANEL):
                rows[k] = rows[k] - lead[k] * rows[i]
        done = jnp.concatenate(rows, axis=0)
        work[pl.ds(base, PANEL), :] = done
        rest = size - base - PANEL
        if rest > 0:
            change = lax.dot_general(
                done[:, :size].T,
                done,
                (((1,), (0,)), ((), ())),
                precision=lax.Precision.HIGHEST,
                preferred_element_type=jnp.float32,
            )
            work[pl.ds(base + PANEL, rest), :] = (
                work[pl.ds(base + PANEL, rest), :] - change[base + PANEL :, :]
            )


def split_two(values):
    high = values.astype(jnp.bfloat16)
    low = (values - high.astype(jnp.float32)).astype(jnp.bfloat16)
    return high, low


def ortho_kernel(scale, gram_ref, filt_ref, ortho_ref, upper_ref, work, filt, out, in_sem, out_sem):
    size = gram_ref.shape[0]
    rows = filt.shape[0]
    fetch = pltpu.make_async_copy(filt_ref, filt, in_sem)
    fetch.start()
    row_id = lax.broadcasted_iota(jnp.int32, (size, size), 0)
    col_id = lax.broadcasted_iota(jnp.int32, (size, size), 1)
    work[:, :size] = gram_ref[...] * scale
    work[:, size:] = jnp.where(row_id == col_id, 1.0, 0.0).astype(jnp.float32)
    factor_panels(work)
    upper_ref[...] = jnp.where(row_id <= col_id, work[:, :size], 0.0)
    high, low = split_two(work[:, size:])
    left = jnp.concatenate(
        [jnp.concatenate([high, high], axis=1), jnp.concatenate([low, low], axis=1)], axis=0
    )
    fetch.wait()
    sends = []
    for group in range(rows // 8):
        parts = []
        for r in range(8):
            both = jnp.dot(left, filt[group * 8 + r], preferred_element_type=jnp.float32)
            parts.append(both[:size] + both[size:])
        out[:, pl.ds(group * 8, 8), :] = jnp.swapaxes(jnp.stack(parts, axis=0), 0, 1)
        send = pltpu.make_async_copy(
            out.at[:, pl.ds(group * 8, 8), :],
            ortho_ref.at[:, pl.ds(group * 8, 8), :],
            out_sem.at[group],
        )
        send.start()
        sends.append(send)
    for send in sends:
        send.wait()


def ortho_call(gram, filt, pixels):
    vectors = gram.shape[0]
    rows, _, cols = filt.shape

    def body(*refs):
        ortho_kernel(1.0 / pixels, *refs)

    return pl.pallas_call(
        body,
        out_shape=(
            jax.ShapeDtypeStruct((vectors, rows, cols), jnp.float32),
            jax.ShapeDtypeStruct((vectors, vectors), jnp.float32),
        ),
        in_specs=[
            pl.BlockSpec(memory_space=pltpu.VMEM),
            pl.BlockSpec(memory_space=pl.ANY),
        ],
        out_specs=(
            pl.BlockSpec(memory_space=pl.ANY),
            pl.BlockSpec(memory_space=pltpu.VMEM),
        ),
        scratch_shapes=[
            pltpu.VMEM((vectors, 2 * vectors), jnp.float32),
            pltpu.VMEM(filt.shape, filt.dtype),
            pltpu.VMEM((vectors, rows, cols), jnp.float32),
            pltpu.SemaphoreType.DMA,
            pltpu.SemaphoreType.DMA((rows // 8,)),
        ],
        compiler_params=pltpu.CompilerParams(vmem_limit_bytes=40 * 1024 * 1024),
        name="ortho",
    )(gram, filt)


def per_device(intensity, agreement, basis_block):
    vectors, tile_rows, tile_cols = basis_block.shape
    row_count = lax.axis_size("row")
    col_count = lax.axis_size("col")
    total_rows = tile_rows * row_count
    total_cols = tile_cols * col_count
    pairs, gram = filter_call(intensity, agreement, basis_block, row_count, col_count)
    return ortho_call(gram, pairs, float(total_rows * total_cols))


def solution(mesh):
    return jax.shard_map(
        per_device,
        mesh=mesh,
        in_specs=(P("row", "col"), P(None, "row", "col"), P(None, "row", "col")),
        out_specs=(P(None, "row", "col"), P()),
        check_vma=False,
    )
```

```python
import jax
import jax.numpy as jnp
from jax import lax
from jax.experimental import pallas as pl
from jax.experimental.pallas import tpu as pltpu
from jax.sharding import PartitionSpec as P

INV_SIGMA = 1.0 / 40.0
NEIGHBOURS = (
    (0, 1, 0, 1, 1.0 / 9.0),
    (0, -1, 0, 0, 1.0 / 9.0),
    (1, 0, 1, 1, 1.0 / 9.0),
    (-1, 0, 1, 0, 1.0 / 9.0),
    (1, 1, 2, 1, 1.0 / 18.0),
    (-1, -1, 2, 0, 1.0 / 18.0),
    (1, -1, 3, 1, 1.0 / 18.0),
    (-1, 1, 3, 0, 1.0 / 18.0),
)
PANEL = 16
VMEM_GRANT = 64 * 1024 * 1024


DIRECTIONS = ((-1, 0), (1, 0), (0, -1), (0, 1), (-1, -1), (-1, 1), (1, -1), (1, 1))
STEPS = ((-1, -1), (0, -1), (1, -1), (-1, 1), (0, 1), (1, 1), (-1, 0), (1, 0))
CHUNK = 16
LANES = 128
EDGE = 8


def moved(array, step_row, step_col):
    height, width = array.shape
    if step_row:
        array = pltpu.roll(array, (-step_row) % height, 0)
    if step_col:
        array = pltpu.roll(array, (-step_col) % width, 1)
    return array


def stencil_weights(levels_ref, counts_ref, weights, row, col, row_count, col_count):
    height, width = levels_ref.shape
    rows, cols = height - 2 * EDGE, width - 2 * LANES
    row_id = lax.broadcasted_iota(jnp.int32, (height, width), 0) - EDGE + row * rows
    col_id = lax.broadcasted_iota(jnp.int32, (height, width), 1) - LANES + col * cols
    total_rows, total_cols = rows * row_count, cols * col_count

    def is_inside(step_row, step_col):
        r, c = row_id + step_row, col_id + step_col
        return (r >= 0) & (r < total_rows) & (c >= 0) & (c < total_cols)

    center_in = is_inside(0, 0)
    levels = levels_ref[...].astype(jnp.float32)
    edges = {}
    for step_row, step_col, channel, at_center, factor in NEIGHBOURS:
        if at_center == 1:
            gap = (levels - moved(levels, step_row, step_col)) * INV_SIGMA
            count = counts_ref[channel].astype(jnp.float32)
            weight = (1.0 + count) * factor * jnp.exp(-gap * gap)
            edges[channel] = (
                jnp.where(center_in & is_inside(step_row, step_col), weight, 0.0),
                (step_row, step_col),
            )
    degree = None
    for step_row, step_col, channel, at_center, factor in NEIGHBOURS:
        weight = edges[channel][0]
        if at_center == 0:
            weight = moved(weight, step_row, step_col)
        degree = weight if degree is None else degree + weight
    scales = lax.rsqrt(1.0 + degree)
    table = {}
    for step_row, step_col, channel, at_center, factor in NEIGHBOURS:
        if at_center == 1:
            scaled = edges[channel][0] * scales * moved(scales, step_row, step_col)
            table[(step_row, step_col)] = scaled
            table[(-step_row, -step_col)] = moved(scaled, -step_row, -step_col)
    lane = lax.broadcasted_iota(jnp.int32, (height, LANES), 1)
    for n, (step_row, step_col) in enumerate(STEPS):
        weight = moved(table[(step_row, step_col)], 0, -step_col)
        weights[n, :, :cols] = weight[:, LANES : LANES + cols]
        weights[n, :, cols:] = jnp.where(
            lane < LANES // 2, weight[:, LANES + cols :], weight[:, :LANES]
        )


def apply_row(source, at, weights, weight_row, store):
    vectors, width = source.shape[1], source.shape[2]
    parts = [weights[n, pl.ds(weight_row, 1), :] for n in range(len(STEPS))]
    for base in range(0, vectors, CHUNK):
        done = []
        for start in range(base, base + CHUNK, 8):
            above = source[at - 1, start : start + 8, :]
            here = source[at, start : start + 8, :]
            below = source[at + 1, start : start + 8, :]
            from_left = parts[0] * above + parts[1] * here + parts[2] * below
            from_right = parts[3] * above + parts[4] * here + parts[5] * below
            upright = parts[6] * above + parts[7] * below
            sides = pltpu.roll(from_left, 1, 1) + pltpu.roll(from_right, width - 1, 1)
            done.append(here - (upright + sides))
        store(base, jnp.concatenate(done, axis=0))


def filter_kernel(
    row_count,
    col_count,
    levels_in,
    counts_in,
    basis_in,
    pair_out,
    gram_out,
    levels,
    counts,
    natural,
    wide,
    middle,
    weights,
    packed,
    halo,
    pairs,
    total,
    share,
    landed,
    blocks,
    whole,
    local_sem,
    send_sem,
    recv_sem,
    sum_send,
    sum_recv,
):
    vectors, rows, cols = natural.shape
    width = cols + LANES
    row, col = lax.axis_index("row"), lax.axis_index("col")

    def device(step_row, step_col):
        return {
            "row": jnp.clip(row + step_row, 0, row_count - 1),
            "col": jnp.clip(col + step_col, 0, col_count - 1),
        }

    def exists(step_row, step_col):
        r, c = row + step_row, col + step_col
        return (r >= 0) & (r < row_count) & (c >= 0) & (c < col_count)

    groups = rows // 8
    order = [0, groups - 1] + list(range(1, groups - 1))
    fetches = {}
    for g in order:
        fetches[g] = pltpu.make_async_copy(
            basis_in.at[:, pl.ds(8 * g, 8), :],
            natural.at[:, pl.ds(8 * g, 8), :],
            local_sem.at[g],
        )
        fetches[g].start()
    own = [
        pltpu.make_async_copy(
            levels_in, levels.at[pl.ds(EDGE, rows), pl.ds(LANES, cols)], local_sem.at[groups]
        ),
        pltpu.make_async_copy(
            counts_in, counts.at[:, pl.ds(EDGE, rows), pl.ds(LANES, cols)], local_sem.at[groups + 1]
        ),
    ]
    for copy in own:
        copy.start()
    zeros = jnp.zeros((2, vectors, cols), jnp.float32)
    wide[0:2, :, :cols] = zeros
    wide[rows + 2 : rows + 4, :, :cols] = zeros
    halo[...] = jnp.zeros(halo.shape, jnp.float32)

    barrier = pltpu.get_barrier_semaphore()

    def greet(target):
        pl.semaphore_signal(
            barrier, inc=1, device_id=target, device_id_type=pl.DeviceIdType.MESH
        )

    for off in range(1, col_count):
        greet({"row": row, "col": lax.rem(col + off, col_count)})
    for off in range(1, row_count):
        greet({"row": lax.rem(row + off, row_count), "col": col})
    corners = jnp.int32(0)
    for step in DIRECTIONS[4:]:
        corners = corners + jnp.where(exists(*step), 1, 0)

        @pl.when(exists(*step))
        def _(step=step):
            greet(device(*step))

    pl.semaphore_wait(barrier, col_count + row_count - 2 + corners)

    def span(step, size, edge):
        if step == 0:
            return 0, edge, size
        if step == 1:
            return size - edge, 0, edge
        return 0, edge + size, edge

    def remote(source, target, kind, d):
        return pltpu.make_async_remote_copy(
            src_ref=source,
            dst_ref=target,
            send_sem=send_sem.at[kind, d],
            recv_sem=recv_sem.at[kind, d],
            device_id=device(*DIRECTIONS[d]),
            device_id_type=pl.DeviceIdType.MESH,
        )

    def launch(d, copies):
        @pl.when(exists(*DIRECTIONS[d]))
        def _():
            for copy in copies:
                copy.start()

    def arrive(d, copies):
        @pl.when(exists(-DIRECTIONS[d][0], -DIRECTIONS[d][1]))
        def _():
            for copy in copies:
                copy.wait_recv()

    label_copies = []
    for d, (step_row, step_col) in enumerate(DIRECTIONS):
        r_from, r_to, r_len = span(step_row, rows, EDGE)
        c_from, c_to, c_len = span(step_col, cols, LANES)
        label_copies.append(
            [
                remote(
                    levels_in.at[pl.ds(r_from, r_len), pl.ds(c_from, c_len)],
                    levels.at[pl.ds(r_to, r_len), pl.ds(c_to, c_len)],
                    0,
                    d,
                ),
                remote(
                    counts_in.at[:, pl.ds(r_from, r_len), pl.ds(c_from, c_len)],
                    counts.at[:, pl.ds(r_to, r_len), pl.ds(c_to, c_len)],
                    1,
                    d,
                ),
            ]
        )
        launch(d, label_copies[d])

    def turn(g):
        fetches[g].wait()
        wide[pl.ds(2 + 8 * g, 8), :, pl.ds(0, cols)] = jnp.swapaxes(
            natural[:, pl.ds(8 * g, 8), :], 0, 1
        )

    turn(0)
    value_copies = [None] * 8
    value_copies[0] = [
        remote(wide.at[pl.ds(2, 2), :, pl.ds(0, cols)],
               wide.at[pl.ds(rows + 2, 2), :, pl.ds(0, cols)], 2, 0)
    ]
    launch(0, value_copies[0])
    turn(groups - 1)
    value_copies[1] = [
        remote(wide.at[pl.ds(rows, 2), :, pl.ds(0, cols)],
               wide.at[pl.ds(0, 2), :, pl.ds(0, cols)], 2, 1)
    ]
    launch(1, value_copies[1])
    for g in range(1, groups - 1):
        turn(g)

    lane = lax.broadcasted_iota(jnp.int32, (vectors, LANES), 1)
    used = 2 * rows
    for side, start in ((0, 0), (1, cols - LANES)):
        gathered = jnp.zeros((vectors, LANES), jnp.float32)
        for r in range(rows):
            strip = wide[2 + r, :, start : start + LANES]
            shift = (2 * r + 2 * side) % LANES
            if shift:
                strip = pltpu.roll(strip, shift, 1)
            gathered = jnp.where(lane // 2 == r, strip, gathered)
        packed[side] = gathered.T
    for d, (step_row, step_col) in enumerate(DIRECTIONS):
        if step_col == 0:
            continue
        side = 0 if step_col < 0 else 1
        p_from, p_to, p_len = span(step_row, used, EDGE)
        value_copies[d] = [
            remote(
                packed.at[side, pl.ds(p_from, p_len), :],
                halo.at[1 - side, pl.ds(p_to, p_len), :],
                2,
                d,
            )
        ]
        launch(d, value_copies[d])

    for copy in own:
        copy.wait()
    for d in range(8):
        arrive(d, label_copies[d])
    stencil_weights(levels, counts, weights, row, col, row_count, col_count)

    def rims(start, stop, left, right):
        for r in range(start, stop):
            on_right = pltpu.roll(right, (-(EDGE + 2 * r)) % LANES, 1)
            on_left = pltpu.roll(left, (LANES - 2 - EDGE - 2 * r) % LANES, 1)
            wide[2 + r, :, cols:] = jnp.where(lane < LANES // 2, on_right, on_left)

    for d in (2, 3):
        arrive(d, value_copies[d])
    above_pad = jnp.zeros((EDGE, vectors), jnp.float32)
    below_pad = jnp.zeros((LANES - EDGE - used, vectors), jnp.float32)
    beside = [
        jnp.concatenate([above_pad, halo[side, pl.ds(EDGE, used), :], below_pad], axis=0).T
        for side in range(2)
    ]
    rims(0, rows, *beside)

    def first(m):
        def store(base, values):
            middle[m, base : base + CHUNK, :] = values

        apply_row(wide, m + 1, weights, m + EDGE - 1, store)

    def second(r):
        def store(base, values):
            high, low = split_two(values[:, :cols])
            pairs[r, base : base + CHUNK, :] = high
            pairs[r, vectors + base : vectors + base + CHUNK, :] = low

        apply_row(middle, r + 1, weights, r + EDGE, store)

    def product(r):
        pair = pairs[r]
        total[...] += lax.dot_general(
            pair, pair, (((1,), (1,)), ((), ())), preferred_element_type=jnp.float32
        )

    total[...] = jnp.zeros(total.shape, jnp.float32)
    first(2)
    first(3)
    first(4)
    second(2)

    first(5)

    def inner(r, carry):
        product(r - 1)
        second(r)
        first(r + 3)
        return carry

    lax.fori_loop(3, rows - 3, inner, 0)
    second(rows - 3)
    product(rows - 4)
    product(rows - 3)
    for d in (0, 1, 4, 5, 6, 7):
        arrive(d, value_copies[d])
    corner = [halo[0].T, halo[1].T]
    rims(-2, 0, *corner)
    rims(rows, rows + 2, *corner)
    for m in (0, 1, rows, rows + 1):
        first(m)
    for r in (0, 1, rows - 2, rows - 1):
        second(r)
    keep = pltpu.make_async_copy(pairs, pair_out, local_sem.at[groups + 2])
    keep.start()
    for r in (0, 1, rows - 2, rows - 1):
        product(r)

    block = vectors // col_count
    share[...] = (total[:vectors, :vectors] + total[vectors:, vectors:]) + (
        total[:vectors, vectors:] + total[vectors:, :vectors]
    )

    def swap(source, target, n, peer):
        copy = pltpu.make_async_remote_copy(
            src_ref=source,
            dst_ref=target,
            send_sem=sum_send.at[n],
            recv_sem=sum_recv.at[n],
            device_id=peer,
            device_id_type=pl.DeviceIdType.MESH,
        )
        copy.start()
        return copy

    def col_peer(off):
        return {"row": row, "col": lax.rem(col + off, col_count)}

    scatter = []
    for off in range(1, col_count):
        place = pl.multiple_of(lax.rem(col + off, col_count) * block, block)
        scatter.append(
            swap(share.at[pl.ds(place, block), :], landed.at[off], off - 1, col_peer(off))
        )
    mine = pl.multiple_of(col * block, block)
    part = share[pl.ds(mine, block), :]
    for off in range(1, col_count):
        scatter[off - 1].wait_recv()
        part = part + landed[off]
    blocks[row] = part
    spread = []
    for off in range(1, row_count):
        spread.append(
            swap(
                blocks.at[row],
                blocks.at[row],
                col_count + off - 1,
                {"row": lax.rem(row + off, row_count), "col": col},
            )
        )
    for copy in spread:
        copy.wait_recv()
    part = blocks[0]
    for n in range(1, row_count):
        part = part + blocks[n]
    whole[pl.ds(mine, block), :] = part
    collect = []
    for off in range(1, col_count):
        collect.append(
            swap(
                whole.at[pl.ds(mine, block), :],
                whole.at[pl.ds(mine, block), :],
                col_count + row_count + off - 1,
                col_peer(off),
            )
        )
    for copy in collect:
        copy.wait_recv()
    gram_out[...] = whole[...]
    for d in range(8):

        @pl.when(exists(*DIRECTIONS[d]))
        def _(d=d):
            for copy in label_copies[d] + value_copies[d]:
                copy.wait_send()

    for copy in scatter + spread + collect:
        copy.wait_send()
    keep.wait()


def filter_call(intensity, agreement, basis_block, row_count, col_count):
    vectors, rows, cols = basis_block.shape
    block = vectors // col_count

    def body(*refs):
        filter_kernel(row_count, col_count, *refs)

    any_spec = pl.BlockSpec(memory_space=pl.ANY)
    f32 = jnp.float32
    swaps = 2 * col_count + row_count
    return pl.pallas_call(
        body,
        out_shape=(
            jax.ShapeDtypeStruct((rows, 2 * vectors, cols), jnp.bfloat16),
            jax.ShapeDtypeStruct((vectors, vectors), f32),
        ),
        in_specs=[any_spec] * 3,
        out_specs=(any_spec, pl.BlockSpec(memory_space=pltpu.VMEM)),
        scratch_shapes=[
            pltpu.VMEM((rows + 2 * EDGE, cols + 2 * LANES), jnp.int32),
            pltpu.VMEM((4, rows + 2 * EDGE, cols + 2 * LANES), jnp.int32),
            pltpu.VMEM((vectors, rows, cols), f32),
            pltpu.VMEM((rows + 4, vectors, cols + LANES), f32),
            pltpu.VMEM((rows + 2, vectors, cols + LANES), f32),
            pltpu.VMEM((len(STEPS), rows + 2 * EDGE, cols + LANES), f32),
            pltpu.VMEM((2, LANES, vectors), f32),
            pltpu.VMEM((2, LANES, vectors), f32),
            pltpu.VMEM((rows, 2 * vectors, cols), jnp.bfloat16),
            pltpu.VMEM((2 * vectors, 2 * vectors), f32),
            pltpu.VMEM((vectors, vectors), f32),
            pltpu.VMEM((col_count, block, vectors), f32),
            pltpu.VMEM((row_count, block, vectors), f32),
            pltpu.VMEM((vectors, vectors), f32),
            pltpu.SemaphoreType.DMA((rows // 8 + 3,)),
            pltpu.SemaphoreType.DMA((3, 8)),
            pltpu.SemaphoreType.DMA((3, 8)),
            pltpu.SemaphoreType.DMA((swaps,)),
            pltpu.SemaphoreType.DMA((swaps,)),
        ],
        compiler_params=pltpu.CompilerParams(
            collective_id=0, has_side_effects=True, vmem_limit_bytes=VMEM_GRANT
        ),
        name="filter",
    )(intensity, agreement, basis_block)


def factor_panels(work):
    size, width = work.shape
    for base in range(0, size, PANEL):
        block = work[pl.ds(base, PANEL), :]
        rows = [block[i : i + 1, :] for i in range(PANEL)]
        pivots = [
            [
                None
                if k < i
                else jnp.broadcast_to(rows[i][:, base + k : base + k + 1], (1, width))
                for k in range(PANEL)
            ]
            for i in range(PANEL)
        ]
        for i in range(PANEL):
            inverse = lax.rsqrt(pivots[i][i])
            rows[i] = rows[i] * inverse
            lead = [None if k <= i else pivots[i][k] * inverse for k in range(PANEL)]
            for k in range(i + 1, PANEL):
                for m in range(k, PANEL):
                    pivots[k][m] = pivots[k][m] - lead[k] * lead[m]
            for k in range(i + 1, PANEL):
                rows[k] = rows[k] - lead[k] * rows[i]
        done = jnp.concatenate(rows, axis=0)
        work[pl.ds(base, PANEL), :] = done
        rest = size - base - PANEL
        if rest > 0:
            change = lax.dot_general(
                done[:, :size].T,
                done,
                (((1,), (0,)), ((), ())),
                precision=lax.Precision.HIGHEST,
                preferred_element_type=jnp.float32,
            )
            work[pl.ds(base + PANEL, rest), :] = (
                work[pl.ds(base + PANEL, rest), :] - change[base + PANEL :, :]
            )


def split_two(values):
    high = values.astype(jnp.bfloat16)
    low = (values - high.astype(jnp.float32)).astype(jnp.bfloat16)
    return high, low


def ortho_kernel(scale, gram_ref, filt_ref, ortho_ref, upper_ref, work, filt, out, in_sem, out_sem):
    size = gram_ref.shape[0]
    rows = filt.shape[0]
    fetch = pltpu.make_async_copy(filt_ref, filt, in_sem)
    fetch.start()
    row_id = lax.broadcasted_iota(jnp.int32, (size, size), 0)
    col_id = lax.broadcasted_iota(jnp.int32, (size, size), 1)
    work[:, :size] = gram_ref[...] * scale
    work[:, size:] = jnp.where(row_id == col_id, 1.0, 0.0).astype(jnp.float32)
    factor_panels(work)
    upper_ref[...] = jnp.where(row_id <= col_id, work[:, :size], 0.0)
    high, low = split_two(work[:, size:])
    left = jnp.concatenate(
        [jnp.concatenate([high, high], axis=1), jnp.concatenate([low, low], axis=1)], axis=0
    )
    fetch.wait()
    sends = []
    for group in range(rows // 8):
        parts = []
        for r in range(8):
            both = jnp.dot(left, filt[group * 8 + r], preferred_element_type=jnp.float32)
            parts.append(both[:size] + both[size:])
        out[:, pl.ds(group * 8, 8), :] = jnp.swapaxes(jnp.stack(parts, axis=0), 0, 1)
        send = pltpu.make_async_copy(
            out.at[:, pl.ds(group * 8, 8), :],
            ortho_ref.at[:, pl.ds(group * 8, 8), :],
            out_sem.at[group],
        )
        send.start()
        sends.append(send)
    for send in sends:
        send.wait()


def ortho_call(gram, filt, pixels):
    vectors = gram.shape[0]
    rows, _, cols = filt.shape

    def body(*refs):
        ortho_kernel(1.0 / pixels, *refs)

    return pl.pallas_call(
        body,
        out_shape=(
            jax.ShapeDtypeStruct((vectors, rows, cols), jnp.float32),
            jax.ShapeDtypeStruct((vectors, vectors), jnp.float32),
        ),
        in_specs=[
            pl.BlockSpec(memory_space=pltpu.VMEM),
            pl.BlockSpec(memory_space=pl.ANY),
        ],
        out_specs=(
            pl.BlockSpec(memory_space=pl.ANY),
            pl.BlockSpec(memory_space=pltpu.VMEM),
        ),
        scratch_shapes=[
            pltpu.VMEM((vectors, 2 * vectors), jnp.float32),
            pltpu.VMEM(filt.shape, filt.dtype),
            pltpu.VMEM((vectors, rows, cols), jnp.float32),
            pltpu.SemaphoreType.DMA,
            pltpu.SemaphoreType.DMA((rows // 8,)),
        ],
        compiler_params=pltpu.CompilerParams(vmem_limit_bytes=VMEM_GRANT),
        name="ortho",
    )(gram, filt)


def per_device(intensity, agreement, basis_block):
    vectors, tile_rows, tile_cols = basis_block.shape
    row_count = lax.axis_size("row")
    col_count = lax.axis_size("col")
    total_rows = tile_rows * row_count
    total_cols = tile_cols * col_count
    pairs, gram = filter_call(intensity, agreement, basis_block, row_count, col_count)
    return ortho_call(gram, pairs, float(total_rows * total_cols))


def solution(mesh):
    return jax.shard_map(
        per_device,
        mesh=mesh,
        in_specs=(P("row", "col"), P(None, "row", "col"), P(None, "row", "col")),
        out_specs=(P(None, "row", "col"), P()),
        check_vma=False,
    )
```

```python
import jax
import jax.numpy as jnp
from jax import lax
from jax.experimental import pallas as pl
from jax.experimental.pallas import tpu as pltpu
from jax.sharding import PartitionSpec as P

INV_SIGMA = 1.0 / 40.0
NEIGHBOURS = (
    (0, 1, 0, 1, 1.0 / 9.0),
    (0, -1, 0, 0, 1.0 / 9.0),
    (1, 0, 1, 1, 1.0 / 9.0),
    (-1, 0, 1, 0, 1.0 / 9.0),
    (1, 1, 2, 1, 1.0 / 18.0),
    (-1, -1, 2, 0, 1.0 / 18.0),
    (1, -1, 3, 1, 1.0 / 18.0),
    (-1, 1, 3, 0, 1.0 / 18.0),
)
PANEL = 16
VMEM_GRANT = 64 * 1024 * 1024


DIRECTIONS = ((-1, 0), (1, 0), (0, -1), (0, 1), (-1, -1), (-1, 1), (1, -1), (1, 1))
STEPS = ((-1, -1), (0, -1), (1, -1), (-1, 1), (0, 1), (1, 1), (-1, 0), (1, 0))
CHUNK = 16
LANES = 128
EDGE = 8


def moved(array, step_row, step_col):
    height, width = array.shape
    if step_row:
        array = pltpu.roll(array, (-step_row) % height, 0)
    if step_col:
        array = pltpu.roll(array, (-step_col) % width, 1)
    return array


def stencil_weights(levels_ref, counts_ref, weights, row, col, row_count, col_count):
    height, width = levels_ref.shape
    rows, cols = height - 2 * EDGE, width - 2 * LANES
    row_id = lax.broadcasted_iota(jnp.int32, (height, width), 0) - EDGE + row * rows
    col_id = lax.broadcasted_iota(jnp.int32, (height, width), 1) - LANES + col * cols
    total_rows, total_cols = rows * row_count, cols * col_count

    def is_inside(step_row, step_col):
        r, c = row_id + step_row, col_id + step_col
        return (r >= 0) & (r < total_rows) & (c >= 0) & (c < total_cols)

    center_in = is_inside(0, 0)
    levels = levels_ref[...].astype(jnp.float32)
    edges = {}
    for step_row, step_col, channel, at_center, factor in NEIGHBOURS:
        if at_center == 1:
            gap = (levels - moved(levels, step_row, step_col)) * INV_SIGMA
            count = counts_ref[channel].astype(jnp.float32)
            weight = (1.0 + count) * factor * jnp.exp(-gap * gap)
            edges[channel] = (
                jnp.where(center_in & is_inside(step_row, step_col), weight, 0.0),
                (step_row, step_col),
            )
    degree = None
    for step_row, step_col, channel, at_center, factor in NEIGHBOURS:
        weight = edges[channel][0]
        if at_center == 0:
            weight = moved(weight, step_row, step_col)
        degree = weight if degree is None else degree + weight
    scales = lax.rsqrt(1.0 + degree)
    table = {}
    for step_row, step_col, channel, at_center, factor in NEIGHBOURS:
        if at_center == 1:
            scaled = edges[channel][0] * scales * moved(scales, step_row, step_col)
            table[(step_row, step_col)] = scaled
            table[(-step_row, -step_col)] = moved(scaled, -step_row, -step_col)
    lane = lax.broadcasted_iota(jnp.int32, (height, LANES), 1)
    for n, (step_row, step_col) in enumerate(STEPS):
        weight = moved(table[(step_row, step_col)], 0, -step_col)
        weights[n, :, :cols] = weight[:, LANES : LANES + cols]
        weights[n, :, cols:] = jnp.where(
            lane < LANES // 2, weight[:, LANES + cols :], weight[:, :LANES]
        )


def apply_row(source, at, weights, weight_row, store):
    vectors, width = source.shape[1], source.shape[2]
    parts = [weights[n, pl.ds(weight_row, 1), :] for n in range(len(STEPS))]
    for base in range(0, vectors, CHUNK):
        done = []
        for start in range(base, base + CHUNK, 8):
            above = source[at - 1, start : start + 8, :]
            here = source[at, start : start + 8, :]
            below = source[at + 1, start : start + 8, :]
            from_left = parts[0] * above + parts[1] * here + parts[2] * below
            from_right = parts[3] * above + parts[4] * here + parts[5] * below
            upright = parts[6] * above + parts[7] * below
            sides = pltpu.roll(from_left, 1, 1) + pltpu.roll(from_right, width - 1, 1)
            done.append(here - (upright + sides))
        store(base, jnp.concatenate(done, axis=0))


def filter_kernel(
    row_count,
    col_count,
    levels_in,
    counts_in,
    basis_in,
    pair_out,
    gram_out,
    levels,
    counts,
    natural,
    wide,
    middle,
    weights,
    packed,
    halo,
    pairs,
    total,
    share,
    landed,
    blocks,
    whole,
    local_sem,
    send_sem,
    recv_sem,
    sum_send,
    sum_recv,
):
    vectors, rows, cols = natural.shape
    width = cols + LANES
    row, col = lax.axis_index("row"), lax.axis_index("col")

    def device(step_row, step_col):
        return {
            "row": jnp.clip(row + step_row, 0, row_count - 1),
            "col": jnp.clip(col + step_col, 0, col_count - 1),
        }

    def exists(step_row, step_col):
        r, c = row + step_row, col + step_col
        return (r >= 0) & (r < row_count) & (c >= 0) & (c < col_count)

    groups = rows // 8
    order = [0, groups - 1] + list(range(1, groups - 1))
    fetches = {}
    for g in order:
        fetches[g] = pltpu.make_async_copy(
            basis_in.at[:, pl.ds(8 * g, 8), :],
            natural.at[:, pl.ds(8 * g, 8), :],
            local_sem.at[g],
        )
        fetches[g].start()
    own = [
        pltpu.make_async_copy(
            levels_in, levels.at[pl.ds(EDGE, rows), pl.ds(LANES, cols)], local_sem.at[groups]
        ),
        pltpu.make_async_copy(
            counts_in, counts.at[:, pl.ds(EDGE, rows), pl.ds(LANES, cols)], local_sem.at[groups + 1]
        ),
    ]
    for copy in own:
        copy.start()
    zeros = jnp.zeros((2, vectors, cols), jnp.float32)
    wide[0:2, :, :cols] = zeros
    wide[rows + 2 : rows + 4, :, :cols] = zeros
    halo[...] = jnp.zeros(halo.shape, jnp.float32)

    barrier = pltpu.get_barrier_semaphore()

    def greet(target):
        pl.semaphore_signal(
            barrier, inc=1, device_id=target, device_id_type=pl.DeviceIdType.MESH
        )

    for off in range(1, col_count):
        greet({"row": row, "col": lax.rem(col + off, col_count)})
    for off in range(1, row_count):
        greet({"row": lax.rem(row + off, row_count), "col": col})
    corners = jnp.int32(0)
    for step in DIRECTIONS[4:]:
        corners = corners + jnp.where(exists(*step), 1, 0)

        @pl.when(exists(*step))
        def _(step=step):
            greet(device(*step))

    pl.semaphore_wait(barrier, col_count + row_count - 2 + corners)

    def span(step, size, edge):
        if step == 0:
            return 0, edge, size
        if step == 1:
            return size - edge, 0, edge
        return 0, edge + size, edge

    def remote(source, target, kind, d):
        return pltpu.make_async_remote_copy(
            src_ref=source,
            dst_ref=target,
            send_sem=send_sem.at[kind, d],
            recv_sem=recv_sem.at[kind, d],
            device_id=device(*DIRECTIONS[d]),
            device_id_type=pl.DeviceIdType.MESH,
        )

    def launch(d, copies):
        @pl.when(exists(*DIRECTIONS[d]))
        def _():
            for copy in copies:
                copy.start()

    def arrive(d, copies):
        @pl.when(exists(-DIRECTIONS[d][0], -DIRECTIONS[d][1]))
        def _():
            for copy in copies:
                copy.wait_recv()

    label_copies = []
    for d, (step_row, step_col) in enumerate(DIRECTIONS):
        r_from, r_to, r_len = span(step_row, rows, EDGE)
        c_from, c_to, c_len = span(step_col, cols, LANES)
        label_copies.append(
            [
                remote(
                    levels_in.at[pl.ds(r_from, r_len), pl.ds(c_from, c_len)],
                    levels.at[pl.ds(r_to, r_len), pl.ds(c_to, c_len)],
                    0,
                    d,
                ),
                remote(
                    counts_in.at[:, pl.ds(r_from, r_len), pl.ds(c_from, c_len)],
                    counts.at[:, pl.ds(r_to, r_len), pl.ds(c_to, c_len)],
                    1,
                    d,
                ),
            ]
        )
        launch(d, label_copies[d])

    def turn(g):
        fetches[g].wait()
        wide[pl.ds(2 + 8 * g, 8), :, pl.ds(0, cols)] = jnp.swapaxes(
            natural[:, pl.ds(8 * g, 8), :], 0, 1
        )

    turn(0)
    value_copies = [None] * 8
    value_copies[0] = [
        remote(wide.at[pl.ds(2, 2), :, pl.ds(0, cols)],
               wide.at[pl.ds(rows + 2, 2), :, pl.ds(0, cols)], 2, 0)
    ]
    launch(0, value_copies[0])
    turn(groups - 1)
    value_copies[1] = [
        remote(wide.at[pl.ds(rows, 2), :, pl.ds(0, cols)],
               wide.at[pl.ds(0, 2), :, pl.ds(0, cols)], 2, 1)
    ]
    launch(1, value_copies[1])
    for g in range(1, groups - 1):
        turn(g)

    lane = lax.broadcasted_iota(jnp.int32, (vectors, LANES), 1)
    used = 2 * rows
    for side, start in ((0, 0), (1, cols - LANES)):
        gathered = jnp.zeros((vectors, LANES), jnp.float32)
        for r in range(rows):
            strip = wide[2 + r, :, start : start + LANES]
            shift = (2 * r + 2 * side) % LANES
            if shift:
                strip = pltpu.roll(strip, shift, 1)
            gathered = jnp.where(lane // 2 == r, strip, gathered)
        packed[side] = gathered.T
    for d, (step_row, step_col) in enumerate(DIRECTIONS):
        if step_col == 0:
            continue
        side = 0 if step_col < 0 else 1
        p_from, p_to, p_len = span(step_row, used, EDGE)
        value_copies[d] = [
            remote(
                packed.at[side, pl.ds(p_from, p_len), :],
                halo.at[1 - side, pl.ds(p_to, p_len), :],
                2,
                d,
            )
        ]
        launch(d, value_copies[d])

    for copy in own:
        copy.wait()
    for d in range(8):
        arrive(d, label_copies[d])
    stencil_weights(levels, counts, weights, row, col, row_count, col_count)

    def rims(start, stop, left, right):
        for r in range(start, stop):
            on_right = pltpu.roll(right, (-(EDGE + 2 * r)) % LANES, 1)
            on_left = pltpu.roll(left, (LANES - 2 - EDGE - 2 * r) % LANES, 1)
            wide[2 + r, :, cols:] = jnp.where(lane < LANES // 2, on_right, on_left)

    for d in (2, 3):
        arrive(d, value_copies[d])
    above_pad = jnp.zeros((EDGE, vectors), jnp.float32)
    below_pad = jnp.zeros((LANES - EDGE - used, vectors), jnp.float32)
    beside = [
        jnp.concatenate([above_pad, halo[side, pl.ds(EDGE, used), :], below_pad], axis=0).T
        for side in range(2)
    ]
    rims(0, rows, *beside)

    def first(m):
        def store(base, values):
            middle[m, base : base + CHUNK, :] = values

        apply_row(wide, m + 1, weights, m + EDGE - 1, store)

    def second(r):
        def store(base, values):
            high, low = split_two(values[:, :cols])
            pairs[r, base : base + CHUNK, :] = high
            pairs[r, vectors + base : vectors + base + CHUNK, :] = low

        apply_row(middle, r + 1, weights, r + EDGE, store)

    def product(r, s):
        pair = jnp.concatenate([pairs[r], pairs[s]], axis=1)
        total[...] += lax.dot_general(
            pair, pair, (((1,), (1,)), ((), ())), preferred_element_type=jnp.float32
        )

    total[...] = jnp.zeros(total.shape, jnp.float32)
    for m in range(2, 6):
        first(m)
    second(2)
    second(3)
    first(6)
    first(7)

    def inner(i, carry):
        r = 4 + 2 * i
        product(r - 2, r - 1)
        second(r)
        second(r + 1)
        first(r + 4)
        first(r + 5)
        return carry

    lax.fori_loop(0, (rows - 8) // 2, inner, 0)
    product(rows - 6, rows - 5)
    second(rows - 4)
    second(rows - 3)
    product(rows - 4, rows - 3)
    for d in (0, 1, 4, 5, 6, 7):
        arrive(d, value_copies[d])
    corner = [halo[0].T, halo[1].T]
    rims(-2, 0, *corner)
    rims(rows, rows + 2, *corner)
    for m in (0, 1, rows, rows + 1):
        first(m)
    for r in (0, 1, rows - 2, rows - 1):
        second(r)
    keep = pltpu.make_async_copy(pairs, pair_out, local_sem.at[groups + 2])
    keep.start()
    product(0, 1)
    product(rows - 2, rows - 1)

    block = vectors // col_count
    share[...] = (total[:vectors, :vectors] + total[vectors:, vectors:]) + (
        total[:vectors, vectors:] + total[vectors:, :vectors]
    )

    def swap(source, target, n, peer):
        copy = pltpu.make_async_remote_copy(
            src_ref=source,
            dst_ref=target,
            send_sem=sum_send.at[n],
            recv_sem=sum_recv.at[n],
            device_id=peer,
            device_id_type=pl.DeviceIdType.MESH,
        )
        copy.start()
        return copy

    def col_peer(off):
        return {"row": row, "col": lax.rem(col + off, col_count)}

    scatter = []
    for off in range(1, col_count):
        place = pl.multiple_of(lax.rem(col + off, col_count) * block, block)
        scatter.append(
            swap(share.at[pl.ds(place, block), :], landed.at[off], off - 1, col_peer(off))
        )
    mine = pl.multiple_of(col * block, block)
    part = share[pl.ds(mine, block), :]
    for off in range(1, col_count):
        scatter[off - 1].wait_recv()
        part = part + landed[off]
    blocks[row] = part
    spread = []
    for off in range(1, row_count):
        spread.append(
            swap(
                blocks.at[row],
                blocks.at[row],
                col_count + off - 1,
                {"row": lax.rem(row + off, row_count), "col": col},
            )
        )
    for copy in spread:
        copy.wait_recv()
    part = blocks[0]
    for n in range(1, row_count):
        part = part + blocks[n]
    whole[pl.ds(mine, block), :] = part
    collect = []
    for off in range(1, col_count):
        collect.append(
            swap(
                whole.at[pl.ds(mine, block), :],
                whole.at[pl.ds(mine, block), :],
                col_count + row_count + off - 1,
                col_peer(off),
            )
        )
    for copy in collect:
        copy.wait_recv()
    gram_out[...] = whole[...]
    for d in range(8):

        @pl.when(exists(*DIRECTIONS[d]))
        def _(d=d):
            for copy in label_copies[d] + value_copies[d]:
                copy.wait_send()

    for copy in scatter + spread + collect:
        copy.wait_send()
    keep.wait()


def filter_call(intensity, agreement, basis_block, row_count, col_count):
    vectors, rows, cols = basis_block.shape
    block = vectors // col_count

    def body(*refs):
        filter_kernel(row_count, col_count, *refs)

    any_spec = pl.BlockSpec(memory_space=pl.ANY)
    f32 = jnp.float32
    swaps = 2 * col_count + row_count
    return pl.pallas_call(
        body,
        out_shape=(
            jax.ShapeDtypeStruct((rows, 2 * vectors, cols), jnp.bfloat16),
            jax.ShapeDtypeStruct((vectors, vectors), f32),
        ),
        in_specs=[any_spec] * 3,
        out_specs=(any_spec, pl.BlockSpec(memory_space=pltpu.VMEM)),
        scratch_shapes=[
            pltpu.VMEM((rows + 2 * EDGE, cols + 2 * LANES), jnp.int32),
            pltpu.VMEM((4, rows + 2 * EDGE, cols + 2 * LANES), jnp.int32),
            pltpu.VMEM((vectors, rows, cols), f32),
            pltpu.VMEM((rows + 4, vectors, cols + LANES), f32),
            pltpu.VMEM((rows + 2, vectors, cols + LANES), f32),
            pltpu.VMEM((len(STEPS), rows + 2 * EDGE, cols + LANES), f32),
            pltpu.VMEM((2, LANES, vectors), f32),
            pltpu.VMEM((2, LANES, vectors), f32),
            pltpu.VMEM((rows, 2 * vectors, cols), jnp.bfloat16),
            pltpu.VMEM((2 * vectors, 2 * vectors), f32),
            pltpu.VMEM((vectors, vectors), f32),
            pltpu.VMEM((col_count, block, vectors), f32),
            pltpu.VMEM((row_count, block, vectors), f32),
            pltpu.VMEM((vectors, vectors), f32),
            pltpu.SemaphoreType.DMA((rows // 8 + 3,)),
            pltpu.SemaphoreType.DMA((3, 8)),
            pltpu.SemaphoreType.DMA((3, 8)),
            pltpu.SemaphoreType.DMA((swaps,)),
            pltpu.SemaphoreType.DMA((swaps,)),
        ],
        compiler_params=pltpu.CompilerParams(
            collective_id=0, has_side_effects=True, vmem_limit_bytes=VMEM_GRANT
        ),
        name="filter",
    )(intensity, agreement, basis_block)


def factor_panels(work):
    size, width = work.shape
    for base in range(0, size, PANEL):
        block = work[pl.ds(base, PANEL), :]
        rows = [
            [block[i : i + 1, side : side + LANES] for side in range(0, width, LANES)]
            for i in range(PANEL)
        ]
        pivots = [
            [
                None
                if k < i
                else jnp.broadcast_to(block[i : i + 1, base + k : base + k + 1], (1, LANES))
                for k in range(PANEL)
            ]
            for i in range(PANEL)
        ]
        for i in range(PANEL):
            inverse = lax.rsqrt(pivots[i][i])
            rows[i] = [half * inverse for half in rows[i]]
            lead = [None if k <= i else pivots[i][k] * inverse for k in range(PANEL)]
            for k in range(i + 1, PANEL):
                for m in range(k, PANEL):
                    pivots[k][m] = pivots[k][m] - lead[k] * lead[m]
            for k in range(i + 1, PANEL):
                rows[k] = [half - lead[k] * done for half, done in zip(rows[k], rows[i])]
        done = jnp.concatenate([jnp.concatenate(halves, axis=1) for halves in rows], axis=0)
        work[pl.ds(base, PANEL), :] = done
        rest = size - base - PANEL
        if rest > 0:
            change = jnp.dot(
                done[:, :size].T[base + PANEL :],
                done,
                precision=lax.Precision.HIGHEST,
                preferred_element_type=jnp.float32,
            )
            work[pl.ds(base + PANEL, rest), :] = work[pl.ds(base + PANEL, rest), :] - change


def split_two(values):
    high = values.astype(jnp.bfloat16)
    low = (values - high.astype(jnp.float32)).astype(jnp.bfloat16)
    return high, low


def ortho_kernel(scale, gram_ref, filt_ref, ortho_ref, upper_ref, work, filt, out, in_sem, out_sem):
    size = gram_ref.shape[0]
    rows = filt.shape[0]
    fetch = pltpu.make_async_copy(filt_ref, filt, in_sem)
    fetch.start()
    row_id = lax.broadcasted_iota(jnp.int32, (size, size), 0)
    col_id = lax.broadcasted_iota(jnp.int32, (size, size), 1)
    work[:, :size] = gram_ref[...] * scale
    work[:, size:] = jnp.where(row_id == col_id, 1.0, 0.0).astype(jnp.float32)
    factor_panels(work)
    upper_ref[...] = jnp.where(row_id <= col_id, work[:, :size], 0.0)
    high, low = split_two(work[:, size:])
    left = jnp.concatenate(
        [jnp.concatenate([high, high], axis=1), jnp.concatenate([low, low], axis=1)], axis=0
    )
    fetch.wait()
    sends = []
    for group in range(rows // 8):
        parts = []
        for r in range(8):
            both = jnp.dot(left, filt[group * 8 + r], preferred_element_type=jnp.float32)
            parts.append(both[:size] + both[size:])
        out[:, pl.ds(group * 8, 8), :] = jnp.swapaxes(jnp.stack(parts, axis=0), 0, 1)
        send = pltpu.make_async_copy(
            out.at[:, pl.ds(group * 8, 8), :],
            ortho_ref.at[:, pl.ds(group * 8, 8), :],
            out_sem.at[group],
        )
        send.start()
        sends.append(send)
    for send in sends:
        send.wait()


def ortho_call(gram, filt, pixels):
    vectors = gram.shape[0]
    rows, _, cols = filt.shape

    def body(*refs):
        ortho_kernel(1.0 / pixels, *refs)

    return pl.pallas_call(
        body,
        out_shape=(
            jax.ShapeDtypeStruct((vectors, rows, cols), jnp.float32),
            jax.ShapeDtypeStruct((vectors, vectors), jnp.float32),
        ),
        in_specs=[
            pl.BlockSpec(memory_space=pltpu.VMEM),
            pl.BlockSpec(memory_space=pl.ANY),
        ],
        out_specs=(
            pl.BlockSpec(memory_space=pl.ANY),
            pl.BlockSpec(memory_space=pltpu.VMEM),
        ),
        scratch_shapes=[
            pltpu.VMEM((vectors, 2 * vectors), jnp.float32),
            pltpu.VMEM(filt.shape, filt.dtype),
            pltpu.VMEM((vectors, rows, cols), jnp.float32),
            pltpu.SemaphoreType.DMA,
            pltpu.SemaphoreType.DMA((rows // 8,)),
        ],
        compiler_params=pltpu.CompilerParams(vmem_limit_bytes=VMEM_GRANT),
        name="ortho",
    )(gram, filt)


def per_device(intensity, agreement, basis_block):
    vectors, tile_rows, tile_cols = basis_block.shape
    row_count = lax.axis_size("row")
    col_count = lax.axis_size("col")
    total_rows = tile_rows * row_count
    total_cols = tile_cols * col_count
    pairs, gram = filter_call(intensity, agreement, basis_block, row_count, col_count)
    return ortho_call(gram, pairs, float(total_rows * total_cols))


def solution(mesh):
    return jax.shard_map(
        per_device,
        mesh=mesh,
        in_specs=(P("row", "col"), P(None, "row", "col"), P(None, "row", "col")),
        out_specs=(P(None, "row", "col"), P()),
        check_vma=False,
    )
```

```python
import jax
import jax.numpy as jnp
from jax import lax
from jax.experimental import pallas as pl
from jax.experimental.pallas import tpu as pltpu
from jax.sharding import PartitionSpec as P

INV_SIGMA = 1.0 / 40.0
NEIGHBOURS = (
    (0, 1, 0, 1, 1.0 / 9.0),
    (0, -1, 0, 0, 1.0 / 9.0),
    (1, 0, 1, 1, 1.0 / 9.0),
    (-1, 0, 1, 0, 1.0 / 9.0),
    (1, 1, 2, 1, 1.0 / 18.0),
    (-1, -1, 2, 0, 1.0 / 18.0),
    (1, -1, 3, 1, 1.0 / 18.0),
    (-1, 1, 3, 0, 1.0 / 18.0),
)
PANEL = 16
VMEM_GRANT = 64 * 1024 * 1024


DIRECTIONS = ((-1, 0), (1, 0), (0, -1), (0, 1), (-1, -1), (-1, 1), (1, -1), (1, 1))
STEPS = ((-1, -1), (0, -1), (1, -1), (-1, 1), (0, 1), (1, 1), (-1, 0), (1, 0))
CHUNK = 16
LANES = 128
EDGE = 8


def moved(array, step_row, step_col):
    height, width = array.shape
    if step_row:
        array = pltpu.roll(array, (-step_row) % height, 0)
    if step_col:
        array = pltpu.roll(array, (-step_col) % width, 1)
    return array


def stencil_weights(levels_ref, counts_ref, weights, row, col, row_count, col_count):
    height, width = levels_ref.shape
    rows, cols = height - 2 * EDGE, width - 2 * LANES
    row_id = lax.broadcasted_iota(jnp.int32, (height, width), 0) - EDGE + row * rows
    col_id = lax.broadcasted_iota(jnp.int32, (height, width), 1) - LANES + col * cols
    total_rows, total_cols = rows * row_count, cols * col_count

    def is_inside(step_row, step_col):
        r, c = row_id + step_row, col_id + step_col
        return (r >= 0) & (r < total_rows) & (c >= 0) & (c < total_cols)

    center_in = is_inside(0, 0)
    levels = levels_ref[...].astype(jnp.float32)
    edges = {}
    for step_row, step_col, channel, at_center, factor in NEIGHBOURS:
        if at_center == 1:
            gap = (levels - moved(levels, step_row, step_col)) * INV_SIGMA
            count = counts_ref[channel].astype(jnp.float32)
            weight = (1.0 + count) * factor * jnp.exp(-gap * gap)
            edges[channel] = (
                jnp.where(center_in & is_inside(step_row, step_col), weight, 0.0),
                (step_row, step_col),
            )
    degree = None
    for step_row, step_col, channel, at_center, factor in NEIGHBOURS:
        weight = edges[channel][0]
        if at_center == 0:
            weight = moved(weight, step_row, step_col)
        degree = weight if degree is None else degree + weight
    scales = lax.rsqrt(1.0 + degree)
    table = {}
    for step_row, step_col, channel, at_center, factor in NEIGHBOURS:
        if at_center == 1:
            scaled = edges[channel][0] * scales * moved(scales, step_row, step_col)
            table[(step_row, step_col)] = scaled
            table[(-step_row, -step_col)] = moved(scaled, -step_row, -step_col)
    lane = lax.broadcasted_iota(jnp.int32, (height, LANES), 1)
    for n, (step_row, step_col) in enumerate(STEPS):
        weight = moved(table[(step_row, step_col)], 0, -step_col)
        weights[n, :, :cols] = weight[:, LANES : LANES + cols]
        weights[n, :, cols:] = jnp.where(
            lane < LANES // 2, weight[:, LANES + cols :], weight[:, :LANES]
        )


def apply_row(source, at, weights, weight_row, store):
    vectors, width = source.shape[1], source.shape[2]
    parts = [weights[n, pl.ds(weight_row, 1), :] for n in range(len(STEPS))]
    for base in range(0, vectors, CHUNK):
        done = []
        for start in range(base, base + CHUNK, 8):
            above = source[at - 1, start : start + 8, :]
            here = source[at, start : start + 8, :]
            below = source[at + 1, start : start + 8, :]
            from_left = parts[0] * above + parts[1] * here + parts[2] * below
            from_right = parts[3] * above + parts[4] * here + parts[5] * below
            upright = parts[6] * above + parts[7] * below
            sides = pltpu.roll(from_left, 1, 1) + pltpu.roll(from_right, width - 1, 1)
            done.append(here - (upright + sides))
        store(base, jnp.concatenate(done, axis=0))


def filter_kernel(
    row_count,
    col_count,
    levels_in,
    counts_in,
    basis_in,
    pair_out,
    gram_out,
    levels,
    counts,
    natural,
    wide,
    middle,
    weights,
    packed,
    halo,
    pairs,
    total,
    share,
    landed,
    blocks,
    whole,
    local_sem,
    send_sem,
    recv_sem,
    sum_send,
    sum_recv,
):
    vectors, rows, cols = natural.shape
    width = cols + LANES
    row, col = lax.axis_index("row"), lax.axis_index("col")

    def device(step_row, step_col):
        return {
            "row": jnp.clip(row + step_row, 0, row_count - 1),
            "col": jnp.clip(col + step_col, 0, col_count - 1),
        }

    def exists(step_row, step_col):
        r, c = row + step_row, col + step_col
        return (r >= 0) & (r < row_count) & (c >= 0) & (c < col_count)

    groups = rows // 8
    order = [0, groups - 1] + list(range(1, groups - 1))
    fetches = {}
    for g in order:
        fetches[g] = pltpu.make_async_copy(
            basis_in.at[:, pl.ds(8 * g, 8), :],
            natural.at[:, pl.ds(8 * g, 8), :],
            local_sem.at[g],
        )
        fetches[g].start()
    own = [
        pltpu.make_async_copy(
            levels_in, levels.at[pl.ds(EDGE, rows), pl.ds(LANES, cols)], local_sem.at[groups]
        ),
        pltpu.make_async_copy(
            counts_in, counts.at[:, pl.ds(EDGE, rows), pl.ds(LANES, cols)], local_sem.at[groups + 1]
        ),
    ]
    for copy in own:
        copy.start()
    zeros = jnp.zeros((2, vectors, cols), jnp.float32)
    wide[0:2, :, :cols] = zeros
    wide[rows + 2 : rows + 4, :, :cols] = zeros
    halo[...] = jnp.zeros(halo.shape, jnp.float32)

    barrier = pltpu.get_barrier_semaphore()

    def greet(target):
        pl.semaphore_signal(
            barrier, inc=1, device_id=target, device_id_type=pl.DeviceIdType.MESH
        )

    for off in range(1, col_count):
        greet({"row": row, "col": lax.rem(col + off, col_count)})
    for off in range(1, row_count):
        greet({"row": lax.rem(row + off, row_count), "col": col})
    corners = jnp.int32(0)
    for step in DIRECTIONS[4:]:
        corners = corners + jnp.where(exists(*step), 1, 0)

        @pl.when(exists(*step))
        def _(step=step):
            greet(device(*step))

    def turn(g):
        fetches[g].wait()
        wide[pl.ds(2 + 8 * g, 8), :, pl.ds(0, cols)] = jnp.swapaxes(
            natural[:, pl.ds(8 * g, 8), :], 0, 1
        )

    turn(0)
    turn(groups - 1)
    pl.semaphore_wait(barrier, col_count + row_count - 2 + corners)

    def span(step, size, edge):
        if step == 0:
            return 0, edge, size
        if step == 1:
            return size - edge, 0, edge
        return 0, edge + size, edge

    def remote(source, target, kind, d):
        return pltpu.make_async_remote_copy(
            src_ref=source,
            dst_ref=target,
            send_sem=send_sem.at[kind, d],
            recv_sem=recv_sem.at[kind, d],
            device_id=device(*DIRECTIONS[d]),
            device_id_type=pl.DeviceIdType.MESH,
        )

    def launch(d, copies):
        @pl.when(exists(*DIRECTIONS[d]))
        def _():
            for copy in copies:
                copy.start()

    def arrive(d, copies):
        @pl.when(exists(-DIRECTIONS[d][0], -DIRECTIONS[d][1]))
        def _():
            for copy in copies:
                copy.wait_recv()

    label_copies = []
    for d, (step_row, step_col) in enumerate(DIRECTIONS):
        r_from, r_to, r_len = span(step_row, rows, EDGE)
        c_from, c_to, c_len = span(step_col, cols, LANES)
        label_copies.append(
            [
                remote(
                    levels_in.at[pl.ds(r_from, r_len), pl.ds(c_from, c_len)],
                    levels.at[pl.ds(r_to, r_len), pl.ds(c_to, c_len)],
                    0,
                    d,
                ),
                remote(
                    counts_in.at[:, pl.ds(r_from, r_len), pl.ds(c_from, c_len)],
                    counts.at[:, pl.ds(r_to, r_len), pl.ds(c_to, c_len)],
                    1,
                    d,
                ),
            ]
        )
        launch(d, label_copies[d])

    value_copies = [None] * 8
    value_copies[0] = [
        remote(wide.at[pl.ds(2, 2), :, pl.ds(0, cols)],
               wide.at[pl.ds(rows + 2, 2), :, pl.ds(0, cols)], 2, 0)
    ]
    launch(0, value_copies[0])
    value_copies[1] = [
        remote(wide.at[pl.ds(rows, 2), :, pl.ds(0, cols)],
               wide.at[pl.ds(0, 2), :, pl.ds(0, cols)], 2, 1)
    ]
    launch(1, value_copies[1])
    for g in range(1, groups - 1):
        turn(g)

    lane = lax.broadcasted_iota(jnp.int32, (vectors, LANES), 1)
    used = 2 * rows
    for side, start in ((0, 0), (1, cols - LANES)):
        gathered = jnp.zeros((vectors, LANES), jnp.float32)
        for r in range(rows):
            strip = wide[2 + r, :, start : start + LANES]
            shift = (2 * r + 2 * side) % LANES
            if shift:
                strip = pltpu.roll(strip, shift, 1)
            gathered = jnp.where(lane // 2 == r, strip, gathered)
        packed[side] = gathered.T
    for d, (step_row, step_col) in enumerate(DIRECTIONS):
        if step_col == 0:
            continue
        side = 0 if step_col < 0 else 1
        p_from, p_to, p_len = span(step_row, used, EDGE)
        value_copies[d] = [
            remote(
                packed.at[side, pl.ds(p_from, p_len), :],
                halo.at[1 - side, pl.ds(p_to, p_len), :],
                2,
                d,
            )
        ]
        launch(d, value_copies[d])

    for copy in own:
        copy.wait()
    for d in range(8):
        arrive(d, label_copies[d])
    stencil_weights(levels, counts, weights, row, col, row_count, col_count)

    def rims(start, stop, left, right):
        for r in range(start, stop):
            on_right = pltpu.roll(right, (-(EDGE + 2 * r)) % LANES, 1)
            on_left = pltpu.roll(left, (LANES - 2 - EDGE - 2 * r) % LANES, 1)
            wide[2 + r, :, cols:] = jnp.where(lane < LANES // 2, on_right, on_left)

    for d in (2, 3):
        arrive(d, value_copies[d])
    above_pad = jnp.zeros((EDGE, vectors), jnp.float32)
    below_pad = jnp.zeros((LANES - EDGE - used, vectors), jnp.float32)
    beside = [
        jnp.concatenate([above_pad, halo[side, pl.ds(EDGE, used), :], below_pad], axis=0).T
        for side in range(2)
    ]
    rims(0, rows, *beside)

    def first(m):
        def store(base, values):
            middle[m, base : base + CHUNK, :] = values

        apply_row(wide, m + 1, weights, m + EDGE - 1, store)

    def second(r):
        def store(base, values):
            high, low = split_two(values[:, :cols])
            pairs[r, base : base + CHUNK, :] = high
            pairs[r, vectors + base : vectors + base + CHUNK, :] = low

        apply_row(middle, r + 1, weights, r + EDGE, store)

    def product(r, s):
        pair = jnp.concatenate([pairs[r], pairs[s]], axis=1)
        total[...] += lax.dot_general(
            pair, pair, (((1,), (1,)), ((), ())), preferred_element_type=jnp.float32
        )

    total[...] = jnp.zeros(total.shape, jnp.float32)
    for m in range(2, 6):
        first(m)
    second(2)
    second(3)
    first(6)
    first(7)

    def inner(i, carry):
        r = 4 + 2 * i
        product(r - 2, r - 1)
        second(r)
        second(r + 1)
        first(r + 4)
        first(r + 5)
        return carry

    lax.fori_loop(0, (rows - 8) // 2, inner, 0)
    product(rows - 6, rows - 5)
    second(rows - 4)
    second(rows - 3)
    product(rows - 4, rows - 3)
    for d in (0, 1, 4, 5, 6, 7):
        arrive(d, value_copies[d])
    corner = [halo[0].T, halo[1].T]
    rims(-2, 0, *corner)
    rims(rows, rows + 2, *corner)
    for m in (0, 1, rows, rows + 1):
        first(m)
    for r in (0, 1, rows - 2, rows - 1):
        second(r)
    keep = pltpu.make_async_copy(pairs, pair_out, local_sem.at[groups + 2])
    keep.start()
    product(0, 1)
    product(rows - 2, rows - 1)

    block = vectors // col_count
    share[...] = (total[:vectors, :vectors] + total[vectors:, vectors:]) + (
        total[:vectors, vectors:] + total[vectors:, :vectors]
    )

    def swap(source, target, n, peer):
        copy = pltpu.make_async_remote_copy(
            src_ref=source,
            dst_ref=target,
            send_sem=sum_send.at[n],
            recv_sem=sum_recv.at[n],
            device_id=peer,
            device_id_type=pl.DeviceIdType.MESH,
        )
        copy.start()
        return copy

    def col_peer(off):
        return {"row": row, "col": lax.rem(col + off, col_count)}

    scatter = []
    for off in range(1, col_count):
        place = pl.multiple_of(lax.rem(col + off, col_count) * block, block)
        scatter.append(
            swap(share.at[pl.ds(place, block), :], landed.at[off], off - 1, col_peer(off))
        )
    mine = pl.multiple_of(col * block, block)
    part = share[pl.ds(mine, block), :]
    for off in range(1, col_count):
        scatter[off - 1].wait_recv()
        part = part + landed[off]
    blocks[row] = part
    spread = []
    for off in range(1, row_count):
        spread.append(
            swap(
                blocks.at[row],
                blocks.at[row],
                col_count + off - 1,
                {"row": lax.rem(row + off, row_count), "col": col},
            )
        )
    for copy in spread:
        copy.wait_recv()
    part = blocks[0]
    for n in range(1, row_count):
        part = part + blocks[n]
    whole[pl.ds(mine, block), :] = part
    collect = []
    for off in range(1, col_count):
        collect.append(
            swap(
                whole.at[pl.ds(mine, block), :],
                whole.at[pl.ds(mine, block), :],
                col_count + row_count + off - 1,
                col_peer(off),
            )
        )
    for copy in collect:
        copy.wait_recv()
    gram_out[...] = whole[...]
    for d in range(8):

        @pl.when(exists(*DIRECTIONS[d]))
        def _(d=d):
            for copy in label_copies[d] + value_copies[d]:
                copy.wait_send()

    for copy in scatter + spread + collect:
        copy.wait_send()
    keep.wait()


def filter_call(intensity, agreement, basis_block, row_count, col_count):
    vectors, rows, cols = basis_block.shape
    block = vectors // col_count

    def body(*refs):
        filter_kernel(row_count, col_count, *refs)

    any_spec = pl.BlockSpec(memory_space=pl.ANY)
    f32 = jnp.float32
    swaps = 2 * col_count + row_count
    return pl.pallas_call(
        body,
        out_shape=(
            jax.ShapeDtypeStruct((rows, 2 * vectors, cols), jnp.bfloat16),
            jax.ShapeDtypeStruct((vectors, vectors), f32),
        ),
        in_specs=[any_spec] * 3,
        out_specs=(any_spec, pl.BlockSpec(memory_space=pltpu.VMEM)),
        scratch_shapes=[
            pltpu.VMEM((rows + 2 * EDGE, cols + 2 * LANES), jnp.int32),
            pltpu.VMEM((4, rows + 2 * EDGE, cols + 2 * LANES), jnp.int32),
            pltpu.VMEM((vectors, rows, cols), f32),
            pltpu.VMEM((rows + 4, vectors, cols + LANES), f32),
            pltpu.VMEM((rows + 2, vectors, cols + LANES), f32),
            pltpu.VMEM((len(STEPS), rows + 2 * EDGE, cols + LANES), f32),
            pltpu.VMEM((2, LANES, vectors), f32),
            pltpu.VMEM((2, LANES, vectors), f32),
            pltpu.VMEM((rows, 2 * vectors, cols), jnp.bfloat16),
            pltpu.VMEM((2 * vectors, 2 * vectors), f32),
            pltpu.VMEM((vectors, vectors), f32),
            pltpu.VMEM((col_count, block, vectors), f32),
            pltpu.VMEM((row_count, block, vectors), f32),
            pltpu.VMEM((vectors, vectors), f32),
            pltpu.SemaphoreType.DMA((rows // 8 + 3,)),
            pltpu.SemaphoreType.DMA((3, 8)),
            pltpu.SemaphoreType.DMA((3, 8)),
            pltpu.SemaphoreType.DMA((swaps,)),
            pltpu.SemaphoreType.DMA((swaps,)),
        ],
        compiler_params=pltpu.CompilerParams(
            collective_id=0, has_side_effects=True, vmem_limit_bytes=VMEM_GRANT
        ),
        name="filter",
    )(intensity, agreement, basis_block)


def factor_panels(work):
    size, width = work.shape
    for base in range(0, size, PANEL):
        block = work[pl.ds(base, PANEL), :]
        rows = [
            [block[i : i + 1, side : side + LANES] for side in range(0, width, LANES)]
            for i in range(PANEL)
        ]
        pivots = [
            [
                None
                if k < i
                else jnp.broadcast_to(block[i : i + 1, base + k : base + k + 1], (1, LANES))
                for k in range(PANEL)
            ]
            for i in range(PANEL)
        ]
        for i in range(PANEL):
            inverse = lax.rsqrt(pivots[i][i])
            rows[i] = [half * inverse for half in rows[i]]
            lead = [None if k <= i else pivots[i][k] * inverse for k in range(PANEL)]
            for k in range(i + 1, PANEL):
                for m in range(k, PANEL):
                    pivots[k][m] = pivots[k][m] - lead[k] * lead[m]
            for k in range(i + 1, PANEL):
                rows[k] = [half - lead[k] * done for half, done in zip(rows[k], rows[i])]
        done = jnp.concatenate([jnp.concatenate(halves, axis=1) for halves in rows], axis=0)
        work[pl.ds(base, PANEL), :] = done
        rest = size - base - PANEL
        if rest > 0:
            change = jnp.dot(
                done[:, :size].T[base + PANEL :],
                done,
                precision=lax.Precision.HIGHEST,
                preferred_element_type=jnp.float32,
            )
            work[pl.ds(base + PANEL, rest), :] = work[pl.ds(base + PANEL, rest), :] - change


def split_two(values):
    high = values.astype(jnp.bfloat16)
    low = (values - high.astype(jnp.float32)).astype(jnp.bfloat16)
    return high, low


def ortho_kernel(scale, gram_ref, filt_ref, ortho_ref, upper_ref, work, filt, out, in_sem, out_sem):
    size = gram_ref.shape[0]
    rows = filt.shape[0]
    fetch = pltpu.make_async_copy(filt_ref, filt, in_sem)
    fetch.start()
    row_id = lax.broadcasted_iota(jnp.int32, (size, size), 0)
    col_id = lax.broadcasted_iota(jnp.int32, (size, size), 1)
    work[:, :size] = gram_ref[...] * scale
    work[:, size:] = jnp.where(row_id == col_id, 1.0, 0.0).astype(jnp.float32)
    factor_panels(work)
    upper_ref[...] = jnp.where(row_id <= col_id, work[:, :size], 0.0)
    high, low = split_two(work[:, size:])
    left = jnp.concatenate(
        [jnp.concatenate([high, high], axis=1), jnp.concatenate([low, low], axis=1)], axis=0
    )
    fetch.wait()
    sends = []
    for group in range(rows // 8):
        parts = []
        for r in range(8):
            both = jnp.dot(left, filt[group * 8 + r], preferred_element_type=jnp.float32)
            parts.append(both[:size] + both[size:])
        out[:, pl.ds(group * 8, 8), :] = jnp.swapaxes(jnp.stack(parts, axis=0), 0, 1)
        send = pltpu.make_async_copy(
            out.at[:, pl.ds(group * 8, 8), :],
            ortho_ref.at[:, pl.ds(group * 8, 8), :],
            out_sem.at[group],
        )
        send.start()
        sends.append(send)
    for send in sends:
        send.wait()


def ortho_call(gram, filt, pixels):
    vectors = gram.shape[0]
    rows, _, cols = filt.shape

    def body(*refs):
        ortho_kernel(1.0 / pixels, *refs)

    return pl.pallas_call(
        body,
        out_shape=(
            jax.ShapeDtypeStruct((vectors, rows, cols), jnp.float32),
            jax.ShapeDtypeStruct((vectors, vectors), jnp.float32),
        ),
        in_specs=[
            pl.BlockSpec(memory_space=pltpu.VMEM),
            pl.BlockSpec(memory_space=pl.ANY),
        ],
        out_specs=(
            pl.BlockSpec(memory_space=pl.ANY),
            pl.BlockSpec(memory_space=pltpu.VMEM),
        ),
        scratch_shapes=[
            pltpu.VMEM((vectors, 2 * vectors), jnp.float32),
            pltpu.VMEM(filt.shape, filt.dtype),
            pltpu.VMEM((vectors, rows, cols), jnp.float32),
            pltpu.SemaphoreType.DMA,
            pltpu.SemaphoreType.DMA((rows // 8,)),
        ],
        compiler_params=pltpu.CompilerParams(vmem_limit_bytes=VMEM_GRANT),
        name="ortho",
    )(gram, filt)


def per_device(intensity, agreement, basis_block):
    vectors, tile_rows, tile_cols = basis_block.shape
    row_count = lax.axis_size("row")
    col_count = lax.axis_size("col")
    total_rows = tile_rows * row_count
    total_cols = tile_cols * col_count
    pairs, gram = filter_call(intensity, agreement, basis_block, row_count, col_count)
    return ortho_call(gram, pairs, float(total_rows * total_cols))


def solution(mesh):
    return jax.shard_map(
        per_device,
        mesh=mesh,
        in_specs=(P("row", "col"), P(None, "row", "col"), P(None, "row", "col")),
        out_specs=(P(None, "row", "col"), P()),
        check_vma=False,
    )
```
